512 devices in a mesh: grp: 32 (over x, y, core), tp: 16 (over z).
Axes of the slice: x: 4, y: 4, z: 16, core: 2. Of those that a mesh axis runs over, the one named last changes fastest.
Arguments:
- queries: bfloat16 [32, 2048, 2048], P('grp', 'tp'), may hold values from -6 to 6
- keys: bfloat16 [32, 2048, 2048], P('grp', 'tp'), may hold values from -6 to 6
- values: bfloat16 [32, 2048, 2048], P('grp', 'tp'), may hold values from -6 to 6
- upstream: bfloat16 [32, 2048, 2048], P('grp', 'tp'), may hold values from -6 to 6
- q_gain: float32 [128], replicated, may hold values from 0.5 to 1.5
- k_gain: float32 [128], replicated, may hold values from 0.5 to 1.5
- segments: int32 [32, 2048], P('grp'), may hold values from 0 to 31, never falling along the last dimension, each value on 1 to 128 neighbouring positions
Outputs:
- attended: bfloat16 [32, 2048, 2048], P('grp', 'tp')
- query_grad: bfloat16 [32, 2048, 2048], P('grp', 'tp')
- key_grad: bfloat16 [32, 2048, 2048], P('grp', 'tp')
- value_grad: bfloat16 [32, 2048, 2048], P('grp', 'tp')
- gain_grads: float32 [2, 128], replicated
The draws below stay inside these ranges and needn't reach their ends.
Inputs may be any that keep to these rules, and one draw needn't show every extreme that they name: In each sequence segment numbers never fall, each of the 32 segments occupies 1 to 128 positions, and some segment occupies exactly 128.
All inputs are finite; a program needn't handle non-finite values.
Results may differ from the reference program's by a relative error of at most 0.012.
Values may be sent and summed in bfloat16 or wider, within the bound.
No kernel may reach another device: no remote copies, remote signals or barrier semaphores. Data moves between devices by JAX's collectives and lax.ppermute only.
A program may use at most 64 MiB of HBM per device.

```python
import math
import jax
import jax.numpy as jnp
import numpy as np
from jax import lax

HD = 128
HEADS = 16
ROWS_DEV = 128
SEQ = 2048
SEQS = 32
COUNT = 32


def block_scale(stream_key, extent, cuts, low, high):
    def one(dim, blocks):
        steps = jax.random.uniform(jax.random.fold_in(jax.random.fold_in(stream_key, 6), dim), (blocks,), jnp.float32, low / len(cuts), high / len(cuts))
        return jnp.repeat(jnp.exp(steps), extent[dim] // blocks).reshape((-1,) + (1,) * (len(extent) - dim - 1))

    level = one(*cuts[0])
    for cut in cuts[1:]:
        level = level * one(*cut)
    return level


def length_profile(count, total, reach, skew):
    weights = [(1 << 20) // math.isqrt(standing ** skew) + 1 for standing in range(2, count + 1)]
    spare, holding = total - reach - (count - 1), [1] * (count - 1)
    while spare > 0:
        candidates = [i for i in range(count - 1) if holding[i] < reach]
        mass, remaining = sum([weights[i] for i in candidates]), spare
        for i in candidates:
            extra = min(reach - holding[i], max(1, remaining * weights[i] // mass), spare)
            holding[i] = holding[i] + extra
            spare = spare - extra
    return np.array([reach] + holding)


def ragged(key, amount, total, bound, slope):
    if amount == 2:
        one = jax.random.randint(key, (), max(1, total - bound), min(bound, total - 1) + 1)
        return jnp.stack([one, total - one])
    lengths = jnp.asarray(length_profile(amount, total, bound, slope), jnp.int32)
    couples = (amount - 1) // 2
    giver, receiver = lengths[1:1 + 2 * couples:2], lengths[2:2 + 2 * couples:2]
    room = jnp.minimum(giver - 1, bound - receiver)
    moved = jax.random.randint(jax.random.fold_in(key, 1), (couples,), 0, 1 << 20) % (room + 1)
    lengths = lengths.at[1:1 + 2 * couples:2].set(giver - moved).at[2:2 + 2 * couples:2].set(receiver + moved)
    return lengths[jax.random.permutation(jax.random.fold_in(key, 2), amount)]


def centred(key, shape, spread, reach, shards=(), held_as=jnp.bfloat16):
    level = block_scale(key, shape, shards, -0.22, 0.18) if shards else 1.0
    values = jax.random.normal(key, shape, jnp.float32) * spread * level
    return jnp.minimum(jnp.maximum(values, -reach), reach).astype(held_as)


def setup_inputs(seed: int = 0) -> dict:
    arg_keys = jax.random.split(jax.random.key(seed), 8)
    queries = centred(arg_keys[0], (SEQS, SEQ, HEADS * HD), 1.0, 6.0, ((0, 32), (1, 16)))
    keys = centred(arg_keys[1], (SEQS, SEQ, HEADS * HD), 1.0, 6.0, ((0, 32), (1, 16)))
    values = centred(arg_keys[2], (SEQS, SEQ, HEADS * HD), 1.0, 6.0, ((0, 32), (1, 16)))
    upstream = centred(arg_keys[3], (SEQS, SEQ, HEADS * HD), 1.0, 6.0, ((0, 32), (1, 16)))
    q_gain = jnp.clip(1.0 + 0.1 * jax.random.normal(arg_keys[4], (HD,), jnp.float32), 0.5, 1.5)
    k_gain = jnp.clip(1.0 + 0.1 * jax.random.normal(arg_keys[5], (HD,), jnp.float32), 0.5, 1.5)
    segments = jax.vmap(lambda own: jnp.searchsorted(jnp.cumsum(ragged(own, COUNT, SEQ, ROWS_DEV, 2)), jnp.arange(SEQ), side="right"))(jax.random.split(arg_keys[6], SEQS)).reshape((SEQS, SEQ)).astype(jnp.int32)
    return {"queries": queries, "keys": keys, "values": values, "upstream": upstream, "q_gain": q_gain, "k_gain": k_gain, "segments": segments}


def normalize(block, gain):
    values_f = block.astype(jnp.float32)
    recip = lax.rsqrt(lax.optimization_barrier(jnp.mean(values_f * values_f, axis=-1, keepdims=True)) + 1e-06)
    unit = values_f * recip
    return (unit, recip, (unit * gain).astype(jnp.bfloat16))

def norm_back(unit, recip, normgrad, gain):
    scaled = normgrad * gain
    inner = lax.optimization_barrier(jnp.mean(scaled * unit, axis=-1, keepdims=True))
    return (recip * (scaled - unit * inner)).astype(jnp.bfloat16)

def attend(query_h, key_h, value_h, grad_h, query_seg, key_seg, scale):
    qf = query_h.astype(jnp.float32)
    kf = key_h.astype(jnp.float32)
    vf = value_h.astype(jnp.float32)
    gf = grad_h.astype(jnp.float32)
    scores = jnp.einsum('qhd,khd->hqk', qf, kf) * scale
    same = (query_seg[:, None] == key_seg[None, :])[None]
    weight = jnp.where(same, jnp.exp(scores), 0.0)
    probs = weight / lax.optimization_barrier(jnp.sum(weight, axis=-1, keepdims=True))
    rounded = probs.astype(jnp.bfloat16)
    rounded_f = rounded.astype(jnp.float32)
    output = jnp.einsum('hqk,khd->qhd', rounded_f, vf)
    dprobs = jnp.einsum('qhd,khd->hqk', gf, vf)
    delta = jnp.einsum('qhd,qhd->hq', gf, output)[..., None]
    dscores = (probs * (dprobs - delta)).astype(jnp.bfloat16).astype(jnp.float32)
    dquery = jnp.einsum('hqk,khd->qhd', dscores, kf) * scale
    dkey = jnp.einsum('hqk,qhd->khd', dscores, qf) * scale
    dvalue = jnp.einsum('hqk,qhd->khd', rounded_f, gf)
    return (output, dquery, dkey, dvalue)

def reference(queries, keys, values, upstream, q_gain, k_gain, segments):
    scale = 1.0 / math.sqrt(HD)
    shape3 = (SEQ, HEADS, HD)

    def one_sequence(items):
        query_s, key_s, value_s, grad_s, seq_ids = items
        q_unit, q_recip, q_norm = normalize(query_s.reshape(shape3), q_gain)
        k_unit, k_recip, k_norm = normalize(key_s.reshape(shape3), k_gain)
        value3 = value_s.reshape(shape3)
        grad3 = grad_s.reshape(shape3)

        def one_head(head_items):
            qh, kh, vh, gh = head_items
            result = attend(qh[:, None], kh[:, None], vh[:, None], gh[:, None], seq_ids, seq_ids, scale)
            return tuple((part[:, 0] for part in result))
        stacked = lax.map(one_head, (q_norm.transpose(1, 0, 2), k_norm.transpose(1, 0, 2), value3.transpose(1, 0, 2), grad3.transpose(1, 0, 2)))
        output, q_normgrad, k_normgrad, dvalue = [part.transpose(1, 0, 2) for part in stacked]
        query_grad = norm_back(q_unit, q_recip, q_normgrad, q_gain)
        key_grad = norm_back(k_unit, k_recip, k_normgrad, k_gain)
        partial_sums = jnp.stack([lax.optimization_barrier(jnp.sum(q_normgrad * q_unit, axis=(0, 1))), lax.optimization_barrier(jnp.sum(k_normgrad * k_unit, axis=(0, 1)))])
        flat = (SEQ, HEADS * HD)
        return (output.astype(jnp.bfloat16).reshape(flat), query_grad.reshape(flat), key_grad.reshape(flat), dvalue.astype(jnp.bfloat16).reshape(flat), partial_sums)
    results = lax.map(one_sequence, (queries, keys, values, upstream, segments))
    gain_grads = lax.optimization_barrier(jnp.sum(results[4], axis=0)) * (1.0 / math.sqrt(SEQS * SEQ * HEADS))
    return (results[0], results[1], results[2], results[3], gain_grads)
```

```python
import functools
import math

import jax
import jax.numpy as jnp
from jax import lax
from jax.experimental import pallas as pl
from jax.experimental.pallas import tpu as pltpu
from jax.sharding import PartitionSpec as P

HD = 128
ROWS = 128
BLK = 16
CAP = 36
PAD = 512
UNROLL = 4
VMEM_BYTES = 40 * 1024 * 1024
F32 = jnp.float32
BF16 = jnp.bfloat16


def boundary(left_row, right_row):
    a = jnp.sum(jnp.where(left_row == right_row[:, :1], 1.0, 0.0)).astype(jnp.int32)
    b = jnp.sum(jnp.where(right_row == left_row[:, ROWS - 1 :], 1.0, 0.0)).astype(jnp.int32)
    return a, b


def plan(a, b, exists, heads):
    crosses = jnp.where(jnp.logical_and(exists, a > 0), 1, 0).astype(jnp.int32)
    a, b = a * crosses, b * crosses
    na, nb = (a + BLK - 1) // BLK, (b + BLK - 1) // BLK
    both = jnp.maximum(na + nb, 1)
    h = (heads * nb + both // 2) // both
    return a, b, na, nb, h * crosses, (heads - h) * crosses


def write_plan(prm_ref, seg_ref, heads):
    me = lax.axis_index("tp")
    last = seg_ref.shape[0] - 1
    own = seg_ref[pl.ds(me, 1), :]
    prev = seg_ref[pl.ds(jnp.maximum(me - 1, 0), 1), :]
    after = seg_ref[pl.ds(jnp.minimum(me + 1, last), 1), :]
    left = plan(*boundary(prev, own), me > 0, heads)
    right = plan(*boundary(own, after), me < last, heads)
    for i, value in enumerate(left + right):
        prm_ref[i] = value
    return left, right


def head_cols(j):
    return pl.ds(pl.multiple_of(j * HD, HD), HD)


def pack_kernel(heads, q_ref, k_ref, v_ref, g_ref, seg_ref, to_prev, to_next, prm_ref):
    left, right = write_plan(prm_ref, seg_ref, heads)
    refs = (q_ref, k_ref, v_ref, g_ref)

    def send(out_ref, count, first_head, first_row, blocks):
        def head(jj, _):
            cols = head_cols(first_head + jj)

            def rows(r, _):
                src = pl.ds(pl.multiple_of(first_row + r * BLK, BLK), BLK)
                dst = pl.ds(pl.multiple_of((jj * blocks + r) * BLK, BLK), BLK)
                for t, ref in enumerate(refs):
                    out_ref[dst, t * HD : (t + 1) * HD] = ref[src, cols]
                return 0

            return lax.fori_loop(0, blocks, rows, 0)

        lax.fori_loop(0, count, head, 0)

    _, _, _, nb, h, rest = left
    send(to_prev, rest, h, 0, nb)
    _, _, na, _, h, _ = right
    send(to_next, h, 0, ROWS - na * BLK, na)


def mm(x, y, dims):
    return lax.dot_general(x, y, (dims, ((), ())), preferred_element_type=F32)


NT = ((1,), (1,))
NN = ((1,), (0,))
TN = ((0,), (0,))


def unit_attention(q, k, v, g, mask, row_ok, q_gain, k_gain, scale):
    def normed(x, gain):
        xf = x.astype(F32)
        recip = lax.rsqrt(jnp.sum(xf * xf, axis=-1, keepdims=True) * (1.0 / HD) + 1e-06)
        unit = xf * recip
        return unit, recip, (unit * gain).astype(BF16)

    def back(unit, recip, grad, gain):
        scaled = grad * (gain * scale)
        inner = jnp.sum(scaled * unit, axis=-1, keepdims=True) * (1.0 / HD)
        return (recip * (scaled - unit * inner)).astype(BF16)

    q_unit, q_recip, q_norm = normed(q, q_gain)
    k_unit, k_recip, k_norm = normed(k, k_gain)
    scores = mm(q_norm, k_norm, NT)
    weight = jnp.where(mask, jnp.exp2(scores * (scale * math.log2(math.e))), 0.0)
    total = jnp.sum(weight, axis=-1, keepdims=True)
    probs = weight * (1.0 / jnp.where(row_ok, total, 1.0))
    rounded = probs.astype(BF16)
    out = mm(rounded, v, NN)
    dprobs = mm(g, v, NT)
    delta = jnp.sum(g.astype(F32) * out, axis=-1, keepdims=True)
    dscores = (probs * (dprobs - delta)).astype(BF16)
    dq = mm(dscores, k_norm, NN)
    dk = mm(dscores, q_norm, TN)
    dv = mm(rounded, g, TN)
    results = (
        out.astype(BF16),
        back(q_unit, q_recip, dq, q_gain),
        back(k_unit, k_recip, dk, k_gain),
        dv.astype(BF16),
    )
    return results, dq * q_unit, dk * k_unit


def fold(x):
    return jnp.sum(x.reshape(ROWS // 8, 8, HD), axis=0)


def row_ids():
    return lax.broadcasted_iota(jnp.int32, (ROWS, 1), 0)


def local_kernel(heads, scale, prm_ref, q_ref, k_ref, v_ref, g_ref, seg_ref, qg_ref, kg_ref, o_ref, dq_ref, dk_ref, dv_ref, sums_ref):
    me = lax.axis_index("tp")
    own = jnp.broadcast_to(seg_ref[pl.ds(me, 1), :].astype(F32), (ROWS, ROWS))
    same = own == own.T
    rows = row_ids()
    whole = jnp.logical_and(rows >= prm_ref[1], rows < ROWS - prm_ref[6])
    q_gain, k_gain = qg_ref[...], kg_ref[...]
    sums_ref[...] = jnp.zeros_like(sums_ref)

    def group(i, _):
        for u in range(UNROLL):
            cols = head_cols(i * UNROLL + u)
            results, gq, gk = unit_attention(
                q_ref[:, cols], k_ref[:, cols], v_ref[:, cols], g_ref[:, cols], same, rows >= 0, q_gain, k_gain, scale
            )
            for ref, value in zip((o_ref, dq_ref, dk_ref, dv_ref), results):
                ref[:, cols] = value
            sums_ref[0:8, :] += fold(jnp.where(whole, gq, 0.0))
            sums_ref[8:16, :] += fold(jnp.where(whole, gk, 0.0))
        return 0

    lax.fori_loop(0, heads // UNROLL, group, 0)


def cross_kernel(heads, scale, prm_ref, q_ref, k_ref, v_ref, g_ref, from_prev, from_next, qg_ref, kg_ref, part_ref,
                 o_ref, dq_ref, dk_ref, dv_ref, to_prev, to_next, gains_ref, in_l, in_r, out_l, out_r, sums):
    size = CAP * BLK
    in_l[PAD : PAD + size, :] = from_prev[...]
    in_r[PAD : PAD + size, :] = from_next[...]
    rows = row_ids()
    cols_id = lax.broadcasted_iota(jnp.int32, (1, ROWS), 1)
    q_gain, k_gain = qg_ref[...], kg_ref[...]
    own_refs = (q_ref, k_ref, v_ref, g_ref)
    res_refs = (o_ref, dq_ref, dk_ref, dv_ref)
    sums[...] = part_ref[...]

    def one(j, a, b, start, in_pad, out_pad, prev_side):
        cols = head_cols(j)
        tail, tail_c = rows >= ROWS - a, cols_id >= ROWS - a
        lead, lead_c = rows < b, cols_id < b
        ok, ok_c = jnp.logical_or(tail, lead), jnp.logical_or(tail_c, lead_c)
        theirs, mine = (tail, lead) if prev_side else (lead, tail)
        window = pl.ds(pl.multiple_of(start, BLK), ROWS)
        merged = [
            jnp.where(theirs, in_pad[window, t * HD : (t + 1) * HD], ref[:, cols]) for t, ref in enumerate(own_refs)
        ]
        results, gq, gk = unit_attention(*merged, jnp.logical_and(ok, ok_c), ok, q_gain, k_gain, scale)
        for t, (ref, value) in enumerate(zip(res_refs, results)):
            ref[:, cols] = jnp.where(mine, value, ref[:, cols])
            out_pad[window, t * HD : (t + 1) * HD] = value
        sums[0:8, :] += fold(gq)
        sums[8:16, :] += fold(gk)

    a, b, na, nb, h, _ = [prm_ref[i] for i in range(6)]
    groups_l = (h + UNROLL - 1) // UNROLL

    def left_group(i, _):
        for u in reversed(range(UNROLL)):
            j = (groups_l - 1 - i) * UNROLL + u
            owned = jnp.where(j < h, 1, 0)
            one(j, a * owned, b * owned, PAD + (j + 1) * na * BLK - ROWS, in_l, out_l, True)
        return 0

    lax.fori_loop(0, groups_l, left_group, 0)

    a2, b2, na2, nb2, h2, rest2 = [prm_ref[6 + i] for i in range(6)]
    first = h2 // UNROLL
    last = jnp.where(rest2 > 0, heads // UNROLL, first)

    def right_group(i, _):
        for u in range(UNROLL):
            j = i * UNROLL + u
            owned = jnp.where(j >= h2, 1, 0)
            one(j, a2 * owned, b2 * owned, PAD + (j - h2) * nb2 * BLK, in_r, out_r, False)
        return 0

    lax.fori_loop(first, last, right_group, 0)
    to_prev[...] = out_l[PAD : PAD + size, :]
    to_next[...] = out_r[PAD : PAD + size, :]
    both = jnp.concatenate(
        [jnp.sum(sums[0:8, :], axis=0, keepdims=True), jnp.sum(sums[8:16, :], axis=0, keepdims=True)], axis=0
    )
    gains_ref[...] = jnp.broadcast_to((both * scale)[None], gains_ref.shape)


def merge_kernel(heads, prm_ref, from_prev, from_next, *refs):
    local, cross, final, (in_l, in_r) = refs[0:4], refs[4:8], refs[8:12], refs[12:14]
    size = CAP * BLK
    in_l[PAD : PAD + size, :] = from_prev[...]
    in_r[PAD : PAD + size, :] = from_next[...]
    rows = row_ids()
    _, b, _, nb, h, _ = [prm_ref[i] for i in range(6)]
    a2, _, na2, _, h2, _ = [prm_ref[6 + i] for i in range(6)]
    lead, tail = rows < b, rows >= ROWS - a2

    def group(i, _):
        for u in range(UNROLL):
            j = i * UNROLL + u
            cols = head_cols(j)
            lead_own = rows < b * jnp.where(j < h, 1, 0)
            tail_own = rows >= ROWS - a2 * jnp.where(j >= h2, 1, 0)
            win_l = pl.ds(pl.multiple_of(PAD + jnp.maximum(j - h, 0) * nb * BLK, BLK), ROWS)
            win_r = pl.ds(pl.multiple_of(PAD + (jnp.minimum(j, h2) + 1) * na2 * BLK - ROWS, BLK), ROWS)
            for t in range(4):
                lanes = slice(t * HD, (t + 1) * HD)
                value = jnp.where(lead, in_l[win_l, lanes], local[t][:, cols])
                value = jnp.where(tail, in_r[win_r, lanes], value)
                final[t][:, cols] = jnp.where(jnp.logical_or(lead_own, tail_own), cross[t][:, cols], value)
        return 0

    lax.fori_loop(0, heads // UNROLL, group, 0)


VM = pl.BlockSpec(memory_space=pltpu.VMEM)
SM = pl.BlockSpec(memory_space=pltpu.SMEM)


def call(body, in_specs, out_specs, out_shape, flops, scratch=()):
    return pl.pallas_call(
        body,
        in_specs=in_specs,
        out_specs=out_specs,
        out_shape=out_shape,
        scratch_shapes=list(scratch),
        compiler_params=pltpu.CompilerParams(vmem_limit_bytes=VMEM_BYTES),
        cost_estimate=pl.CostEstimate(flops=flops, bytes_accessed=1 << 22, transcendentals=0),
    )


def per_device(queries, keys, values, upstream, q_gain, k_gain, segments):
    rows, width = queries.shape[1:]
    heads = width // HD
    scale = 1.0 / math.sqrt(HD)
    groups, ring = lax.axis_size("grp"), lax.axis_size("tp")
    args = (queries[0], keys[0], values[0], upstream[0])
    seg = segments[0].reshape(ring, rows)
    gains = (q_gain.reshape(1, HD), k_gain.reshape(1, HD))
    full = jax.ShapeDtypeStruct((rows, width), BF16)
    sent = jax.ShapeDtypeStruct((CAP * BLK, 4 * HD), BF16)
    pad = pltpu.VMEM((CAP * BLK + 2 * PAD, 4 * HD), BF16)
    up = [(i, i + 1) for i in range(ring - 1)]
    down = [(i + 1, i) for i in range(ring - 1)]

    to_prev, to_next, prm = call(
        functools.partial(pack_kernel, heads),
        [VM] * 5,
        [VM, VM, SM],
        [sent, sent, jax.ShapeDtypeStruct((12,), jnp.int32)],
        1 << 20,
    )(*args, seg)
    from_prev = lax.ppermute(to_next, "tp", up)
    from_next = lax.ppermute(to_prev, "tp", down)
    *local, part = call(
        functools.partial(local_kernel, heads, scale),
        [SM] + [VM] * 7,
        [VM] * 5,
        [full] * 4 + [jax.ShapeDtypeStruct((16, HD), F32)],
        1 << 30,
    )(prm, *args, seg, *gains)
    *cross, back_prev, back_next, sums = call(
        functools.partial(cross_kernel, heads, scale),
        [SM] + [VM] * 9,
        [VM] * 7,
        [full] * 4 + [sent, sent, jax.ShapeDtypeStruct((groups, 2, HD), F32)],
        1 << 30,
        [pad] * 4 + [pltpu.VMEM((16, HD), F32)],
    )(prm, *args, from_prev, from_next, *gains, part)
    done_next = lax.ppermute(back_prev, "tp", down)
    done_prev = lax.ppermute(back_next, "tp", up)
    sums = jnp.sum(lax.all_to_all(sums, "grp", 0, 0), axis=0)
    sums = jnp.sum(lax.all_to_all(jnp.broadcast_to(sums, (ring, 2, HD)), "tp", 0, 0), axis=0)
    gain_grads = sums * (1.0 / math.sqrt(groups * ring * rows * heads))
    outs = call(
        functools.partial(merge_kernel, heads),
        [SM] + [VM] * 10,
        [VM] * 4,
        [full] * 4,
        1 << 20,
        [pad] * 2,
    )(prm, done_prev, done_next, *local, *cross)
    return tuple(x[None] for x in outs) + (gain_grads,)


def solution(mesh):
    row = P("grp", "tp", None)
    in_specs = (row, row, row, row, P(), P(), P("grp", None))
    out_specs = (row, row, row, row, P())
    return jax.shard_map(per_device, mesh=mesh, in_specs=in_specs, out_specs=out_specs, check_vma=False)
```

```python
import functools
import math

import jax
import jax.numpy as jnp
from jax import lax
from jax.experimental import pallas as pl
from jax.experimental.pallas import tpu as pltpu
from jax.sharding import PartitionSpec as P

HD = 128
ROWS = 128
BLK = 16
BATCH = 8
CAPS = (20, 16)
FIRST, SECOND = CAPS[0] * BLK, CAPS[1] * BLK
MIB = 1024 * 1024
F32 = jnp.float32
BF16 = jnp.bfloat16


def padded(size):
    return ROWS, 2 * ROWS + size, 2 * (ROWS + size), 3 * ROWS + 2 * size


def most(blocks):
    first = jnp.minimum(CAPS[0] // jnp.maximum(blocks, 1), BATCH)
    return first, first + CAPS[1] // jnp.maximum(blocks, 1)


def plan(left_row, right_row, exists, heads):
    a = jnp.sum(jnp.where(left_row == right_row[:, :1], 1.0, 0.0)).astype(jnp.int32)
    b = jnp.sum(jnp.where(right_row == left_row[:, ROWS - 1 :], 1.0, 0.0)).astype(jnp.int32)
    crosses = jnp.where(jnp.logical_and(exists, a > 0), 1, 0).astype(jnp.int32)
    a, b = a * crosses, b * crosses
    na, nb = (a + BLK - 1) // BLK, (b + BLK - 1) // BLK
    first_a, all_a = most(na)
    first_b, all_b = most(nb)
    h = jnp.minimum(jnp.maximum(heads // 2, heads - all_b), all_a)
    rest = (heads - h) * crosses
    h = h * crosses
    return a, b, na, nb, h, rest, jnp.minimum(h, first_a), jnp.minimum(rest, first_b)


def write_plan(prm_ref, seg_ref, heads):
    me = lax.axis_index("tp")
    last = seg_ref.shape[0] - 1
    own = seg_ref[pl.ds(me, 1), :]
    prev = seg_ref[pl.ds(jnp.maximum(me - 1, 0), 1), :]
    after = seg_ref[pl.ds(jnp.minimum(me + 1, last), 1), :]
    left = plan(prev, own, me > 0, heads)
    right = plan(own, after, me < last, heads)
    for i, value in enumerate(left + right):
        prm_ref[i] = value
    return left, right


def head_cols(j):
    return pl.ds(pl.multiple_of(j * HD, HD), HD)


def pack_kernel(heads, q_hbm, k_hbm, v_hbm, g_hbm, seg_hbm, to_prev, to_next, to_prev2, to_next2, prm_ref, q_ref, k_ref, v_ref, g_ref, seg_ref, sem):
    refs = (q_ref, k_ref, v_ref, g_ref)
    step = ROWS // 4
    copies = []
    first = pltpu.make_async_copy(seg_hbm, seg_ref, sem.at[16])
    first.start()
    for t, (src, dst) in enumerate(zip((q_hbm, k_hbm, v_hbm, g_hbm), refs)):
        for r in range(4):
            part = pl.ds(r * step, step)
            copies.append(pltpu.make_async_copy(src.at[part, :], dst.at[part, :], sem.at[t * 4 + r]))
            copies[-1].start()
    first.wait()
    left, right = write_plan(prm_ref, seg_ref, heads)
    for copy in copies:
        copy.wait()

    def send(out_ref, count, first_head, first_row, blocks):
        def head(jj, _):
            cols = head_cols(first_head + jj)

            def rows(r, _):
                src = pl.ds(pl.multiple_of(first_row + r * BLK, BLK), BLK)
                dst = pl.ds(pl.multiple_of((jj * blocks + r) * BLK, BLK), BLK)
                for t, ref in enumerate(refs):
                    out_ref[dst, t * HD : (t + 1) * HD] = ref[src, cols]
                return 0

            return lax.fori_loop(0, blocks, rows, 0)

        lax.fori_loop(0, count, head, 0)

    _, _, _, nb, h, rest, _, one = left
    _, _, na, _, h2, _, one2, _ = right
    send(to_prev, one, h, 0, nb)
    send(to_next, one2, 0, ROWS - na * BLK, na)
    send(to_prev2, rest - one, h + one, 0, nb)
    send(to_next2, h2 - one2, one2, ROWS - na * BLK, na)


def mm(x, y, dims):
    return lax.dot_general(x, y, (dims, ((), ())), preferred_element_type=F32)


NT = ((1,), (1,))
NN = ((1,), (0,))
TN = ((0,), (0,))


def averager():
    r = lax.broadcasted_iota(jnp.int32, (2 * HD, 2 * HD), 0) // HD
    c = lax.broadcasted_iota(jnp.int32, (2 * HD, 2 * HD), 1) // HD
    return jnp.where(r == c, 1.0 / HD, 0.0).astype(BF16)


def units_attention(items, q_gain, k_gain, scale, mean_of):
    n = range(len(items))
    q, k, v, g, mask, row_ok = zip(*items)

    def means(x, y):
        both = [mm(jnp.concatenate([x[i].astype(BF16), y[i].astype(BF16)], axis=1), mean_of, NN) for i in n]
        return [b[:, :HD] for b in both], [b[:, HD:] for b in both]

    qf, kf = [x.astype(F32) for x in q], [x.astype(F32) for x in k]
    q_mean, k_mean = means([x * x for x in qf], [x * x for x in kf])
    q_recip, k_recip = [lax.rsqrt(x + 1e-06) for x in q_mean], [lax.rsqrt(x + 1e-06) for x in k_mean]
    q_unit, k_unit = [qf[i] * q_recip[i] for i in n], [kf[i] * k_recip[i] for i in n]
    q_norm, k_norm = [(x * q_gain).astype(BF16) for x in q_unit], [(x * k_gain).astype(BF16) for x in k_unit]
    scores = [mm(q_norm[i], k_norm[i], NT) for i in n]
    weight = [
        jnp.where(mask[i], jnp.exp2(scores[i] * (scale * math.log2(math.e))), 0.0).astype(BF16) for i in n
    ]
    ones = jnp.ones((ROWS, HD), BF16)
    sums = [mm(weight[i], jnp.concatenate([v[i], ones], axis=1), NN) for i in n]
    total = [x[:, HD:] for x in sums]
    total = [t if ok is None else jnp.where(ok, t, 1.0) for t, ok in zip(total, row_ok)]
    recip = [1.0 / t for t in total]
    out = [sums[i][:, :HD] * recip[i] for i in n]
    g_part = [g[i].astype(F32) * recip[i] for i in n]
    g_both = [jnp.concatenate([g_part[i].astype(BF16), (g_part[i] * out[i]).astype(BF16)], axis=1) for i in n]
    dprobs = [mm(g_both[i], jnp.concatenate([v[i], -ones], axis=1), NT) for i in n]
    dscores = [(weight[i].astype(F32) * dprobs[i]).astype(BF16) for i in n]
    dv = [mm(weight[i], g_both[i][:, :HD], TN) for i in n]
    dq = [mm(dscores[i], k_norm[i], NN) for i in n]
    dk = [mm(dscores[i], q_norm[i], TN) for i in n]
    q_scaled, k_scaled = [x * (q_gain * scale) for x in dq], [x * (k_gain * scale) for x in dk]
    q_part, k_part = [q_scaled[i] * q_unit[i] for i in n], [k_scaled[i] * k_unit[i] for i in n]
    q_inner, k_inner = means(q_part, k_part)
    results = [
        (
            out[i].astype(BF16),
            (q_recip[i] * (q_scaled[i] - q_unit[i] * q_inner[i])).astype(BF16),
            (k_recip[i] * (k_scaled[i] - k_unit[i] * k_inner[i])).astype(BF16),
            dv[i].astype(BF16),
        )
        for i in n
    ]
    return results, q_part, k_part


def fold(x):
    return jnp.sum(x.reshape(ROWS // 8, 8, HD), axis=0)


def row_ids():
    return lax.broadcasted_iota(jnp.int32, (ROWS, 1), 0)


def local_kernel(heads, scale, prm_ref, q_ref, k_ref, v_ref, g_ref, seg_ref, qg_ref, kg_ref, o_ref, dq_ref, dk_ref, dv_ref, sums_ref):
    me = lax.axis_index("tp")
    own = jnp.broadcast_to(seg_ref[pl.ds(me, 1), :].astype(F32), (ROWS, ROWS))
    same = own == own.T
    rows = row_ids()
    whole = jnp.logical_and(rows >= prm_ref[1], rows < ROWS - prm_ref[8])
    q_gain, k_gain = qg_ref[...], kg_ref[...]
    mean_of = averager()
    sums_ref[...] = jnp.zeros_like(sums_ref)

    def group(i, _):
        cols = [head_cols(i * BATCH + u) for u in range(BATCH)]
        items = [(q_ref[:, c], k_ref[:, c], v_ref[:, c], g_ref[:, c], same, None) for c in cols]
        results, gq, gk = units_attention(items, q_gain, k_gain, scale, mean_of)
        for c, res in zip(cols, results):
            for ref, value in zip((o_ref, dq_ref, dk_ref, dv_ref), res):
                ref[:, c] = value
        sums_ref[0:8, :] += fold(jnp.where(whole, sum(gq), 0.0))
        sums_ref[8:16, :] += fold(jnp.where(whole, sum(gk), 0.0))
        return 0

    lax.fori_loop(0, heads // BATCH, group, 0)


def cross_kernel(heads, second, prm_ref, *refs):
    own, (from_prev, from_next, qg_ref, kg_ref, part_ref), local, refs = refs[0:4], refs[4:9], refs[9:13], refs[13:]
    if second:
        (first_prev, first_next), refs = refs[0:2], refs[2:]
    final, (to_prev, to_next, gains_ref, in_pad, out_pad, sums) = refs[0:4], refs[4:]
    size = from_prev.shape[0]
    left, right, spare, _ = padded(size)
    in_pad[left : left + size, :] = from_prev[...]
    in_pad[right : right + size, :] = from_next[...]
    for src, dst in zip(local, final):
        dst[...] = src[...]
    sums[...] = part_ref[...]
    rows = row_ids()
    cols_id = lax.broadcasted_iota(jnp.int32, (1, ROWS), 1)
    q_gain, k_gain = qg_ref[...], kg_ref[...]
    mean_of = averager()
    a_l, b_l, na_l, _, h_l, _, one_l, _ = [prm_ref[i] for i in range(8)]
    a_r, b_r, _, nb_r, h_r, rest_r, _, one_r = [prm_ref[8 + i] for i in range(8)]
    if second:
        base_l, num_l, base_r, num_r = one_l, h_l - one_l, h_r + one_r, rest_r - one_r
    else:
        base_l, num_l, base_r, num_r = 0, one_l, h_r, one_r
    count = num_l + num_r

    def group(i, _):
        items, places = [], []
        for u in range(BATCH):
            s = i * BATCH + u
            is_l, used = s < num_l, s < count
            n = jnp.where(is_l, num_l - 1 - s, jnp.where(used, s - num_l, 0))
            j = n + jnp.where(is_l, base_l, jnp.where(used, base_r, 0))
            start = jnp.where(
                is_l, left + (n + 1) * na_l * BLK - ROWS, jnp.where(used, right + n * nb_r * BLK, spare)
            )
            a = jnp.where(is_l, a_l, jnp.where(used, a_r, 0))
            b = jnp.where(is_l, b_l, jnp.where(used, b_r, 0))
            ok = jnp.logical_or(rows >= ROWS - a, rows < b)
            ok_c = jnp.logical_or(cols_id >= ROWS - a, cols_id < b)
            low = jnp.where(is_l, ROWS - a, 0)
            high = jnp.where(is_l, ROWS, b)
            theirs = jnp.logical_and(rows >= low, rows < high)
            mine = jnp.logical_and(ok, jnp.logical_not(theirs))
            cols = head_cols(j)
            window = pl.ds(pl.multiple_of(start, BLK), ROWS)
            merged = [
                jnp.where(theirs, in_pad[window, t * HD : (t + 1) * HD], ref[:, cols]) for t, ref in enumerate(own)
            ]
            items.append((*merged, jnp.logical_and(ok, ok_c), ok))
            places.append((cols, window, mine))
        results, gq, gk = units_attention(items, q_gain, k_gain, 1.0 / math.sqrt(HD), mean_of)
        for (cols, window, mine), res in zip(places, results):
            for t, (ref, value) in enumerate(zip(final, res)):
                ref[:, cols] = jnp.where(mine, value, ref[:, cols])
                out_pad[window, t * HD : (t + 1) * HD] = value
        sums[0:8, :] += fold(sum(gq))
        sums[8:16, :] += fold(sum(gk))
        return 0

    lax.fori_loop(0, (count + BATCH - 1) // BATCH, group, 0)
    if not second:
        to_prev[...] = out_pad[left : left + size, :]
        to_next[...] = out_pad[right : right + size, :]
        gains_ref[...] = sums[...]
        return
    for out_ref, start, first in ((to_prev, left, first_prev), (to_next, right, first_next)):
        out_ref[:FIRST, :] = first[...]
        out_ref[FIRST:, :] = out_pad[start : start + size, :]
    both = jnp.concatenate(
        [
            jnp.sum(sums[0:8, :], axis=0, keepdims=True) / q_gain,
            jnp.sum(sums[8:16, :], axis=0, keepdims=True) / k_gain,
        ],
        axis=0,
    )
    gains_ref[...] = jnp.broadcast_to(both[None], gains_ref.shape)


def merge_kernel(heads, prm_ref, from_prev, from_next, *refs):
    local, final, pad = refs[0:4], refs[4:8], refs[8]
    step = pl.program_id(0)

    left, right, _, _ = padded(FIRST + SECOND)

    @pl.when(step == 0)
    def _():
        pad[left : left + FIRST + SECOND, :] = from_prev[...]
        pad[right : right + FIRST + SECOND, :] = from_next[...]

    rows = row_ids()
    _, b, _, nb, h, _, _, one = [prm_ref[i] for i in range(8)]
    a, _, na, _, h2, _, one2, _ = [prm_ref[8 + i] for i in range(8)]
    each = local[0].shape[1] // HD
    for u in range(each):
        j = step * each + u
        lead = rows < b * jnp.where(j >= h, 1, 0)
        tail = rows >= ROWS - a * jnp.where(j < h2, 1, 0)
        n, n2 = jnp.maximum(j - h, 0), jnp.minimum(j, jnp.maximum(h2 - 1, 0))
        at = left + jnp.where(n < one, n * nb * BLK, FIRST + (n - one) * nb * BLK)
        at2 = right + jnp.where(n2 < one2, n2 + 1, n2 + 1 - one2) * na * BLK - ROWS + jnp.where(n2 < one2, 0, FIRST)
        win_l, win_r = pl.ds(pl.multiple_of(at, BLK), ROWS), pl.ds(pl.multiple_of(at2, BLK), ROWS)
        cols = slice(u * HD, (u + 1) * HD)
        for t in range(4):
            lanes = slice(t * HD, (t + 1) * HD)
            value = jnp.where(lead, pad[win_l, lanes], local[t][:, cols])
            final[t][:, cols] = jnp.where(tail, pad[win_r, lanes], value)


VM = pl.BlockSpec(memory_space=pltpu.VMEM)
SM = pl.BlockSpec(memory_space=pltpu.SMEM)
HB = pl.BlockSpec(memory_space=pltpu.HBM)


def call(body, in_specs, out_specs, out_shape, flops, scratch=(), grid=(), vmem=40):
    return pl.pallas_call(
        body,
        grid=grid,
        in_specs=in_specs,
        out_specs=out_specs,
        out_shape=out_shape,
        scratch_shapes=list(scratch),
        compiler_params=pltpu.CompilerParams(vmem_limit_bytes=vmem * MIB),
        cost_estimate=pl.CostEstimate(flops=flops, bytes_accessed=1 << 22, transcendentals=0),
    )


def local_call(heads, args):
    rows, width = args[1].shape
    return call(
        functools.partial(local_kernel, heads, 1.0 / math.sqrt(HD)),
        [SM] + [VM] * 7,
        [VM] * 5,
        [jax.ShapeDtypeStruct((rows, width), BF16)] * 4 + [jax.ShapeDtypeStruct((16, HD), F32)],
        1 << 30,
    )(*args)


def per_device(queries, keys, values, upstream, q_gain, k_gain, segments):
    rows, width = queries.shape[1:]
    heads = width // HD
    groups, ring = lax.axis_size("grp"), lax.axis_size("tp")
    args = (queries[0], keys[0], values[0], upstream[0])
    seg = segments[0].reshape(ring, rows)
    gains = (q_gain.reshape(1, HD), k_gain.reshape(1, HD))
    full = jax.ShapeDtypeStruct((rows, width), BF16)
    sent, sent2, back = [jax.ShapeDtypeStruct((n, 4 * HD), BF16) for n in (FIRST, SECOND, FIRST + SECOND)]
    part = jax.ShapeDtypeStruct((16, HD), F32)
    up = [(i, i + 1) for i in range(ring - 1)]
    down = [(i + 1, i) for i in range(ring - 1)]

    def pad(size):
        return pltpu.VMEM((padded(size)[3], 4 * HD), BF16)

    to_prev, to_next, to_prev2, to_next2, prm, *args, seg = call(
        functools.partial(pack_kernel, heads),
        [HB] * 5,
        [VM] * 4 + [SM] + [VM] * 5,
        [sent, sent, sent2, sent2, jax.ShapeDtypeStruct((16,), jnp.int32)]
        + [full] * 4
        + [jax.ShapeDtypeStruct(seg.shape, seg.dtype)],
        1 << 20,
        [pltpu.SemaphoreType.DMA((17,))],
        vmem=12,
    )(*[pltpu.with_memory_space_constraint(x, pltpu.HBM) for x in (*args, seg)])
    from_prev = lax.ppermute(to_next, "tp", up)
    from_next = lax.ppermute(to_prev, "tp", down)
    from_prev2 = lax.ppermute(to_next2, "tp", up)
    from_next2 = lax.ppermute(to_prev2, "tp", down)
    *local, sums = local_call(heads, (prm, *args, seg, *gains))
    *merged, first_prev, first_next, sums = call(
        functools.partial(cross_kernel, heads, False),
        [SM] + [VM] * 13,
        [VM] * 7,
        [full] * 4 + [sent, sent, part],
        1 << 30,
        [pad(FIRST), pad(FIRST), pltpu.VMEM((16, HD), F32)],
    )(prm, *args, from_prev, from_next, *gains, sums, *local)
    *merged, back_prev, back_next, sums = call(
        functools.partial(cross_kernel, heads, True),
        [SM] + [VM] * 15,
        [VM] * 7,
        [full] * 4 + [back, back, jax.ShapeDtypeStruct((groups, 2, HD), F32)],
        1 << 30,
        [pad(SECOND), pad(SECOND), pltpu.VMEM((16, HD), F32)],
    )(prm, *args, from_prev2, from_next2, *gains, sums, *merged, first_prev, first_next)
    done_next = lax.ppermute(back_prev, "tp", down)
    done_prev = lax.ppermute(back_next, "tp", up)
    sums = jnp.sum(lax.all_to_all(sums, "grp", 0, 0), axis=0)
    block = pl.BlockSpec((rows, width // 4), lambda i: (0, i))
    whole = pl.BlockSpec((FIRST + SECOND, 4 * HD), lambda i: (0, 0))
    outs = call(
        functools.partial(merge_kernel, heads),
        [SM, whole, whole] + [block] * 4,
        [block] * 4,
        [full] * 4,
        1 << 20,
        [pad(FIRST + SECOND)],
        (4,),
        16,
    )(prm, done_prev, done_next, *merged)
    sums = jnp.sum(lax.all_to_all(jnp.broadcast_to(sums, (ring, 2, HD)), "tp", 0, 0), axis=0)
    gain_grads = sums * (1.0 / math.sqrt(groups * ring * rows * heads))
    return tuple(x[None] for x in outs) + (gain_grads,)


def solution(mesh):
    row = P("grp", "tp", None)
    in_specs = (row, row, row, row, P(), P(), P("grp", None))
    out_specs = (row, row, row, row, P())
    return jax.shard_map(per_device, mesh=mesh, in_specs=in_specs, out_specs=out_specs, check_vma=False)
```

```python
import functools
import math

import jax
import jax.numpy as jnp
from jax import lax
from jax.experimental import pallas as pl
from jax.experimental.pallas import tpu as pltpu
from jax.sharding import PartitionSpec as P

HD = 128
ROWS = 128
BLK = 16
BATCH = 8
CAP = 36
SIZE = CAP * BLK
MIB = 1024 * 1024
F32 = jnp.float32
BF16 = jnp.bfloat16


def plan(left_row, right_row, exists, heads):
    a = jnp.sum(jnp.where(left_row == right_row[:, :1], 1.0, 0.0)).astype(jnp.int32)
    b = jnp.sum(jnp.where(right_row == left_row[:, ROWS - 1 :], 1.0, 0.0)).astype(jnp.int32)
    crosses = jnp.where(jnp.logical_and(exists, a > 0), 1, 0).astype(jnp.int32)
    a, b = a * crosses, b * crosses
    na, nb = (a + BLK - 1) // BLK, (b + BLK - 1) // BLK
    h = jnp.maximum(heads // 2, heads - CAP // jnp.maximum(nb, 1))
    h = jnp.minimum(h, CAP // jnp.maximum(na, 1))
    return a, b, na, nb, h * crosses, (heads - h) * crosses


def write_plan(prm_ref, seg_ref, heads):
    me = lax.axis_index("tp")
    last = seg_ref.shape[0] - 1
    own = seg_ref[pl.ds(me, 1), :]
    prev = seg_ref[pl.ds(jnp.maximum(me - 1, 0), 1), :]
    after = seg_ref[pl.ds(jnp.minimum(me + 1, last), 1), :]
    left = plan(prev, own, me > 0, heads)
    right = plan(own, after, me < last, heads)
    both = []
    for x in range(2):
        is_left = lax.rem(me + x, 2)
        both.append([is_left] + [jnp.where(is_left == 1, p, q) for p, q in zip(left, right)])
        for i, value in enumerate(both[x]):
            prm_ref[8 * x + i] = value
    prm_ref[7] = left[1]
    prm_ref[15] = right[0]
    return both


def head_cols(j):
    return pl.ds(pl.multiple_of(j * HD, HD), HD)


def pack_kernel(heads, q_hbm, k_hbm, v_hbm, g_hbm, seg_hbm, out_ref, out_ref2, prm_ref, q_ref, k_ref, v_ref, g_ref, seg_ref, sem):
    refs = (q_ref, k_ref, v_ref, g_ref)
    step = ROWS // 4
    copies = []
    first = pltpu.make_async_copy(seg_hbm, seg_ref, sem.at[16])
    first.start()
    for t, (src, dst) in enumerate(zip((q_hbm, k_hbm, v_hbm, g_hbm), refs)):
        for r in range(4):
            part = pl.ds(r * step, step)
            copies.append(pltpu.make_async_copy(src.at[part, :], dst.at[part, :], sem.at[t * 4 + r]))
            copies[-1].start()
    first.wait()
    plans = write_plan(prm_ref, seg_ref, heads)
    for copy in copies:
        copy.wait()

    for out, (is_left, _, _, na, nb, h, rest) in zip((out_ref, out_ref2), plans):
        count = jnp.where(is_left == 1, rest, h)
        blocks = jnp.where(is_left == 1, nb, na)
        first_head = jnp.where(is_left == 1, h, 0)
        first_row = jnp.where(is_left == 1, 0, ROWS - na * BLK)

        def head(jj, _):
            cols = head_cols(first_head + jj)

            def rows(r, _):
                src = pl.ds(pl.multiple_of(first_row + r * BLK, BLK), BLK)
                dst = pl.ds(pl.multiple_of((jj * blocks + r) * BLK, BLK), BLK)
                for t, ref in enumerate(refs):
                    out[dst, t * HD : (t + 1) * HD] = ref[src, cols]
                return 0

            return lax.fori_loop(0, blocks, rows, 0)

        lax.fori_loop(0, count, head, 0)


def mm(x, y, dims):
    return lax.dot_general(x, y, (dims, ((), ())), preferred_element_type=F32)


NT = ((1,), (1,))
NN = ((1,), (0,))
TN = ((0,), (0,))


def averager():
    r = lax.broadcasted_iota(jnp.int32, (2 * HD, 2 * HD), 0) // HD
    c = lax.broadcasted_iota(jnp.int32, (2 * HD, 2 * HD), 1) // HD
    return jnp.where(r == c, 1.0 / HD, 0.0).astype(BF16)


def units_attention(items, q_gain, k_gain, scale, mean_of):
    n = range(len(items))
    q, k, v, g, mask, row_ok = zip(*items)

    def means(x, y):
        both = [mm(jnp.concatenate([x[i].astype(BF16), y[i].astype(BF16)], axis=1), mean_of, NN) for i in n]
        return [b[:, :HD] for b in both], [b[:, HD:] for b in both]

    qf, kf = [x.astype(F32) for x in q], [x.astype(F32) for x in k]
    q_mean, k_mean = means([x * x for x in qf], [x * x for x in kf])
    q_recip, k_recip = [lax.rsqrt(x + 1e-06) for x in q_mean], [lax.rsqrt(x + 1e-06) for x in k_mean]
    q_unit, k_unit = [qf[i] * q_recip[i] for i in n], [kf[i] * k_recip[i] for i in n]
    q_norm, k_norm = [(x * q_gain).astype(BF16) for x in q_unit], [(x * k_gain).astype(BF16) for x in k_unit]
    scores = [mm(q_norm[i], k_norm[i], NT) for i in n]
    weight = [
        jnp.where(mask[i], jnp.exp2(scores[i] * (scale * math.log2(math.e))), 0.0).astype(BF16) for i in n
    ]
    ones = jnp.ones((ROWS, HD), BF16)
    sums = [mm(weight[i], jnp.concatenate([v[i], ones], axis=1), NN) for i in n]
    total = [x[:, HD:] for x in sums]
    total = [t if ok is None else jnp.where(ok, t, 1.0) for t, ok in zip(total, row_ok)]
    recip = [1.0 / t for t in total]
    out = [sums[i][:, :HD] * recip[i] for i in n]
    g_part = [g[i].astype(F32) * recip[i] for i in n]
    g_both = [jnp.concatenate([g_part[i].astype(BF16), (g_part[i] * out[i]).astype(BF16)], axis=1) for i in n]
    dprobs = [mm(g_both[i], jnp.concatenate([v[i], -ones], axis=1), NT) for i in n]
    dscores = [(weight[i].astype(F32) * dprobs[i]).astype(BF16) for i in n]
    dv = [mm(weight[i], g_both[i][:, :HD], TN) for i in n]
    dq = [mm(dscores[i], k_norm[i], NN) for i in n]
    dk = [mm(dscores[i], q_norm[i], TN) for i in n]
    q_scaled, k_scaled = [x * (q_gain * scale) for x in dq], [x * (k_gain * scale) for x in dk]
    q_part, k_part = [q_scaled[i] * q_unit[i] for i in n], [k_scaled[i] * k_unit[i] for i in n]
    q_inner, k_inner = means(q_part, k_part)
    results = [
        (
            out[i].astype(BF16),
            (q_recip[i] * (q_scaled[i] - q_unit[i] * q_inner[i])).astype(BF16),
            (k_recip[i] * (k_scaled[i] - k_unit[i] * k_inner[i])).astype(BF16),
            dv[i].astype(BF16),
        )
        for i in n
    ]
    return results, q_part, k_part


def fold(x):
    return jnp.sum(x.reshape(ROWS // 8, 8, HD), axis=0)


def row_ids():
    return lax.broadcasted_iota(jnp.int32, (ROWS, 1), 0)


def local_kernel(heads, scale, prm_ref, q_ref, k_ref, v_ref, g_ref, seg_ref, qg_ref, kg_ref, o_ref, dq_ref, dk_ref, dv_ref, sums_ref):
    me = lax.axis_index("tp")
    own = jnp.broadcast_to(seg_ref[pl.ds(me, 1), :].astype(F32), (ROWS, ROWS))
    same = own == own.T
    rows = row_ids()
    whole = jnp.logical_and(rows >= prm_ref[7], rows < ROWS - prm_ref[15])
    q_gain, k_gain = qg_ref[...], kg_ref[...]
    mean_of = averager()
    sums_ref[...] = jnp.zeros_like(sums_ref)

    def group(i, _):
        cols = [head_cols(i * BATCH + u) for u in range(BATCH)]
        items = [(q_ref[:, c], k_ref[:, c], v_ref[:, c], g_ref[:, c], same, None) for c in cols]
        results, gq, gk = units_attention(items, q_gain, k_gain, scale, mean_of)
        for c, res in zip(cols, results):
            for ref, value in zip((o_ref, dq_ref, dk_ref, dv_ref), res):
                ref[:, c] = value
        sums_ref[0:8, :] += fold(jnp.where(whole, sum(gq), 0.0))
        sums_ref[8:16, :] += fold(jnp.where(whole, sum(gk), 0.0))
        return 0

    lax.fori_loop(0, heads // BATCH, group, 0)


def cross_kernel(heads, x, prm_ref, *refs):
    own, (received, qg_ref, kg_ref, part_ref), local = refs[0:4], refs[4:8], refs[8:12]
    final, (back, gains_ref, in_pad, out_pad, sums) = refs[12:16], refs[16:]
    in_pad[ROWS : ROWS + SIZE, :] = received[...]
    for src, dst in zip(local, final):
        dst[...] = src[...]
    sums[...] = part_ref[...]
    rows = row_ids()
    cols_id = lax.broadcasted_iota(jnp.int32, (1, ROWS), 1)
    q_gain, k_gain = qg_ref[...], kg_ref[...]
    mean_of = averager()
    is_left, a_all, b_all, na, nb, h, rest = [prm_ref[8 * x + i] for i in range(7)]
    is_l = is_left == 1
    count = jnp.where(is_l, h, rest)

    def group(i, _):
        items, places = [], []
        for u in range(BATCH):
            s = i * BATCH + u
            used = s < count
            n = jnp.where(used, jnp.where(is_l, count - 1 - s, s), 0)
            j = n + jnp.where(is_l, 0, h)
            start = jnp.where(is_l, ROWS + (n + 1) * na * BLK - ROWS, ROWS + n * nb * BLK)
            start = jnp.where(used, start, ROWS + SIZE)
            a, b = jnp.where(used, a_all, 0), jnp.where(used, b_all, 0)
            ok = jnp.logical_or(rows >= ROWS - a, rows < b)
            ok_c = jnp.logical_or(cols_id >= ROWS - a, cols_id < b)
            low = jnp.where(is_l, ROWS - a, 0)
            high = jnp.where(is_l, ROWS, b)
            theirs = jnp.logical_and(rows >= low, rows < high)
            mine = jnp.logical_and(ok, jnp.logical_not(theirs))
            cols = head_cols(j)
            window = pl.ds(pl.multiple_of(start, BLK), ROWS)
            merged = [
                jnp.where(theirs, in_pad[window, t * HD : (t + 1) * HD], ref[:, cols]) for t, ref in enumerate(own)
            ]
            items.append((*merged, jnp.logical_and(ok, ok_c), ok))
            places.append((cols, window, mine))
        results, gq, gk = units_attention(items, q_gain, k_gain, 1.0 / math.sqrt(HD), mean_of)
        for (cols, window, mine), res in zip(places, results):
            for t, (ref, value) in enumerate(zip(final, res)):
                ref[:, cols] = jnp.where(mine, value, ref[:, cols])
                out_pad[window, t * HD : (t + 1) * HD] = value
        sums[0:8, :] += fold(sum(gq))
        sums[8:16, :] += fold(sum(gk))
        return 0

    lax.fori_loop(0, (count + BATCH - 1) // BATCH, group, 0)
    back[...] = out_pad[ROWS : ROWS + SIZE, :]
    if x == 0:
        gains_ref[...] = sums[...]
        return
    both = jnp.concatenate(
        [
            jnp.sum(sums[0:8, :], axis=0, keepdims=True) / q_gain,
            jnp.sum(sums[8:16, :], axis=0, keepdims=True) / k_gain,
        ],
        axis=0,
    )
    gains_ref[...] = jnp.broadcast_to(both[None], gains_ref.shape)


def merge_kernel(heads, prm_ref, done, done2, *refs):
    local, final, pad = refs[0:4], refs[4:8], refs[8]
    step = pl.program_id(0)
    bases = (ROWS, 2 * ROWS + SIZE)

    @pl.when(step == 0)
    def _():
        for base, ref in zip(bases, (done, done2)):
            pad[base : base + SIZE, :] = ref[...]

    rows = row_ids()
    each = local[0].shape[1] // HD
    for u in range(each):
        j = step * each + u
        cols = slice(u * HD, (u + 1) * HD)
        parts = []
        for x, base in enumerate(bases):
            is_left, a, b, na, nb, h, _ = [prm_ref[8 * x + i] for i in range(7)]
            is_l = is_left == 1
            sent = jnp.where(is_l, j - h, h - 1 - j) >= 0
            n = jnp.where(sent, jnp.where(is_l, j - h, j + 1), 0)
            at = base + jnp.where(is_l, n * nb * BLK, n * na * BLK - ROWS)
            low = jnp.where(is_l, 0, ROWS - a)
            high = jnp.where(sent, jnp.where(is_l, b, ROWS), 0)
            parts.append((pl.ds(pl.multiple_of(at, BLK), ROWS), jnp.logical_and(rows >= low, rows < high)))
        for t in range(4):
            value = local[t][:, cols]
            for window, mask in parts:
                value = jnp.where(mask, pad[window, t * HD : (t + 1) * HD], value)
            final[t][:, cols] = value


VM = pl.BlockSpec(memory_space=pltpu.VMEM)
SM = pl.BlockSpec(memory_space=pltpu.SMEM)
HB = pl.BlockSpec(memory_space=pltpu.HBM)


def call(body, in_specs, out_specs, out_shape, flops, scratch=(), grid=(), vmem=40):
    return pl.pallas_call(
        body,
        grid=grid,
        in_specs=in_specs,
        out_specs=out_specs,
        out_shape=out_shape,
        scratch_shapes=list(scratch),
        compiler_params=pltpu.CompilerParams(vmem_limit_bytes=vmem * MIB),
        cost_estimate=pl.CostEstimate(flops=flops, bytes_accessed=1 << 22, transcendentals=0),
    )


def local_call(heads, args):
    rows, width = args[1].shape
    return call(
        functools.partial(local_kernel, heads, 1.0 / math.sqrt(HD)),
        [SM] + [VM] * 7,
        [VM] * 5,
        [jax.ShapeDtypeStruct((rows, width), BF16)] * 4 + [jax.ShapeDtypeStruct((16, HD), F32)],
        1 << 30,
    )(*args)


def per_device(queries, keys, values, upstream, q_gain, k_gain, segments):
    rows, width = queries.shape[1:]
    heads = width // HD
    groups, ring = lax.axis_size("grp"), lax.axis_size("tp")
    args = (queries[0], keys[0], values[0], upstream[0])
    seg = segments[0].reshape(ring, rows)
    gains = (q_gain.reshape(1, HD), k_gain.reshape(1, HD))
    full = jax.ShapeDtypeStruct((rows, width), BF16)
    sent = jax.ShapeDtypeStruct((SIZE, 4 * HD), BF16)
    part = jax.ShapeDtypeStruct((16, HD), F32)
    pad = pltpu.VMEM((SIZE + 2 * ROWS, 4 * HD), BF16)
    even, odd = [[(i, i + 1) for i in range(x, ring - 1, 2)] + [(i + 1, i) for i in range(x, ring - 1, 2)] for x in range(2)]

    out, out2, prm, *args, seg = call(
        functools.partial(pack_kernel, heads),
        [HB] * 5,
        [VM, VM, SM] + [VM] * 5,
        [sent, sent, jax.ShapeDtypeStruct((16,), jnp.int32)] + [full] * 4 + [jax.ShapeDtypeStruct(seg.shape, seg.dtype)],
        1 << 20,
        [pltpu.SemaphoreType.DMA((17,))],
        vmem=12,
    )(*[pltpu.with_memory_space_constraint(x, pltpu.HBM) for x in (*args, seg)])
    received = lax.ppermute(out, "tp", even)
    received2 = lax.ppermute(out2, "tp", odd)
    *local, sums = local_call(heads, (prm, *args, seg, *gains))

    def cross(x, received, sums, local):
        return call(
            functools.partial(cross_kernel, heads, x),
            [SM] + [VM] * 12,
            [VM] * 6,
            [full] * 4 + [sent, jax.ShapeDtypeStruct((groups, 2, HD), F32) if x else part],
            1 << 30,
            [pad, pad, pltpu.VMEM((16, HD), F32)],
        )(prm, *args, received, *gains, sums, *local)

    *merged, back, sums = cross(0, received, sums, local)
    done = lax.ppermute(back, "tp", even)
    *merged, back2, sums = cross(1, received2, sums, merged)
    done2 = lax.ppermute(back2, "tp", odd)
    sums = jnp.sum(lax.all_to_all(sums, "grp", 0, 0), axis=0)
    block = pl.BlockSpec((rows, width // 4), lambda i: (0, i))
    whole = pl.BlockSpec((SIZE, 4 * HD), lambda i: (0, 0))
    outs = call(
        functools.partial(merge_kernel, heads),
        [SM, whole, whole] + [block] * 4,
        [block] * 4,
        [full] * 4,
        1 << 20,
        [pltpu.VMEM((2 * SIZE + 3 * ROWS, 4 * HD), BF16)],
        (4,),
        16,
    )(prm, done, done2, *merged)
    sums = jnp.sum(lax.all_to_all(jnp.broadcast_to(sums, (ring, 2, HD)), "tp", 0, 0), axis=0)
    gain_grads = sums * (1.0 / math.sqrt(groups * ring * rows * heads))
    return tuple(x[None] for x in outs) + (gain_grads,)


def solution(mesh):
    row = P("grp", "tp", None)
    in_specs = (row, row, row, row, P(), P(), P("grp", None))
    out_specs = (row, row, row, row, P())
    return jax.shard_map(per_device, mesh=mesh, in_specs=in_specs, out_specs=out_specs, check_vma=False)
```

```python
import functools
import math

import jax
import jax.numpy as jnp
from jax import lax
from jax.experimental import pallas as pl
from jax.experimental.pallas import tpu as pltpu
from jax.sharding import PartitionSpec as P

HD = 128
ROWS = 128
BLK = 16
BATCH = 8
MOST = 12
CAP = 36
SIZE = CAP * BLK
MIB = 1024 * 1024
F32 = jnp.float32
BF16 = jnp.bfloat16


def plan(left_row, right_row, exists, heads):
    a = jnp.sum(jnp.where(left_row == right_row[:, :1], 1.0, 0.0)).astype(jnp.int32)
    b = jnp.sum(jnp.where(right_row == left_row[:, ROWS - 1 :], 1.0, 0.0)).astype(jnp.int32)
    crosses = jnp.where(jnp.logical_and(exists, a > 0), 1, 0).astype(jnp.int32)
    a, b = a * crosses, b * crosses
    na, nb = (a + BLK - 1) // BLK, (b + BLK - 1) // BLK
    h = jnp.maximum(heads // 2, heads - CAP // jnp.maximum(nb, 1))
    h = jnp.minimum(h, CAP // jnp.maximum(na, 1))
    return a, b, na, nb, h * crosses, (heads - h) * crosses


def write_plan(prm_ref, seg_ref, heads):
    me = lax.axis_index("tp")
    last = seg_ref.shape[0] - 1
    own = seg_ref[pl.ds(me, 1), :]
    prev = seg_ref[pl.ds(jnp.maximum(me - 1, 0), 1), :]
    after = seg_ref[pl.ds(jnp.minimum(me + 1, last), 1), :]
    left = plan(prev, own, me > 0, heads)
    right = plan(own, after, me < last, heads)
    both = []
    for x in range(2):
        is_left = lax.rem(me + x, 2)
        both.append([is_left] + [jnp.where(is_left == 1, p, q) for p, q in zip(left, right)])
        for i, value in enumerate(both[x]):
            prm_ref[8 * x + i] = value
    prm_ref[7] = left[1]
    prm_ref[15] = right[0]
    return both


def head_cols(j):
    return pl.ds(pl.multiple_of(j * HD, HD), HD)


def pack_kernel(heads, q_hbm, k_hbm, v_hbm, g_hbm, seg_hbm, out_ref, out_ref2, prm_ref, q_ref, k_ref, v_ref, g_ref, seg_ref, sem):
    refs = (q_ref, k_ref, v_ref, g_ref)
    step = ROWS // 4
    copies = []
    first = pltpu.make_async_copy(seg_hbm, seg_ref, sem.at[16])
    first.start()
    for t, (src, dst) in enumerate(zip((q_hbm, k_hbm, v_hbm, g_hbm), refs)):
        for r in range(4):
            part = pl.ds(r * step, step)
            copies.append(pltpu.make_async_copy(src.at[part, :], dst.at[part, :], sem.at[t * 4 + r]))
            copies[-1].start()
    first.wait()
    plans = write_plan(prm_ref, seg_ref, heads)
    for copy in copies:
        copy.wait()

    for out, (is_left, _, _, na, nb, h, rest) in zip((out_ref, out_ref2), plans):
        count = jnp.where(is_left == 1, rest, h)
        blocks = jnp.where(is_left == 1, nb, na)
        first_head = jnp.where(is_left == 1, h, 0)
        first_row = jnp.where(is_left == 1, 0, ROWS - na * BLK)

        def head(jj, _):
            cols = head_cols(first_head + jj)

            def rows(r, _):
                src = pl.ds(pl.multiple_of(first_row + r * BLK, BLK), BLK)
                dst = pl.ds(pl.multiple_of((jj * blocks + r) * BLK, BLK), BLK)
                for t, ref in enumerate(refs):
                    out[dst, t * HD : (t + 1) * HD] = ref[src, cols]
                return 0

            return lax.fori_loop(0, blocks, rows, 0)

        lax.fori_loop(0, count, head, 0)


def mm(x, y, dims):
    return lax.dot_general(x, y, (dims, ((), ())), preferred_element_type=F32)


NT = ((1,), (1,))
NN = ((1,), (0,))
TN = ((0,), (0,))


def averager():
    r = lax.broadcasted_iota(jnp.int32, (2 * HD, 2 * HD), 0) // HD
    c = lax.broadcasted_iota(jnp.int32, (2 * HD, 2 * HD), 1) // HD
    return jnp.where(r == c, 1.0 / HD, 0.0).astype(BF16)


def units_attention(items, q_gain, k_gain, scale, mean_of):
    n = range(len(items))
    q, k, v, g, mask, row_ok = zip(*items)

    def means(x, y):
        both = [mm(jnp.concatenate([x[i].astype(BF16), y[i].astype(BF16)], axis=1), mean_of, NN) for i in n]
        return [b[:, :HD] for b in both], [b[:, HD:] for b in both]

    qf, kf = [x.astype(F32) for x in q], [x.astype(F32) for x in k]
    q_mean, k_mean = means([x * x for x in qf], [x * x for x in kf])
    q_recip, k_recip = [lax.rsqrt(x + 1e-06) for x in q_mean], [lax.rsqrt(x + 1e-06) for x in k_mean]
    q_unit, k_unit = [qf[i] * q_recip[i] for i in n], [kf[i] * k_recip[i] for i in n]
    q_norm, k_norm = [(x * q_gain).astype(BF16) for x in q_unit], [(x * k_gain).astype(BF16) for x in k_unit]
    scores = [mm(q_norm[i], k_norm[i], NT) for i in n]
    weight = [
        jnp.where(mask[i], jnp.exp2(scores[i] * (scale * math.log2(math.e))), 0.0).astype(BF16) for i in n
    ]
    ones = jnp.ones((ROWS, HD), BF16)
    sums = [mm(weight[i], jnp.concatenate([v[i], ones], axis=1), NN) for i in n]
    total = [x[:, HD:] for x in sums]
    total = [t if ok is None else jnp.where(ok, t, 1.0) for t, ok in zip(total, row_ok)]
    recip = [1.0 / t for t in total]
    out = [sums[i][:, :HD] * recip[i] for i in n]
    g_part = [g[i].astype(F32) * recip[i] for i in n]
    g_both = [jnp.concatenate([g_part[i].astype(BF16), (g_part[i] * out[i]).astype(BF16)], axis=1) for i in n]
    dprobs = [mm(g_both[i], jnp.concatenate([v[i], -ones], axis=1), NT) for i in n]
    dscores = [(weight[i].astype(F32) * dprobs[i]).astype(BF16) for i in n]
    dv = [mm(weight[i], g_both[i][:, :HD], TN) for i in n]
    dq = [mm(dscores[i], k_norm[i], NN) for i in n]
    dk = [mm(dscores[i], q_norm[i], TN) for i in n]
    q_scaled, k_scaled = [x * (q_gain * scale) for x in dq], [x * (k_gain * scale) for x in dk]
    q_part, k_part = [q_scaled[i] * q_unit[i] for i in n], [k_scaled[i] * k_unit[i] for i in n]
    q_inner, k_inner = means(q_part, k_part)
    results = [
        (
            out[i].astype(BF16),
            (q_recip[i] * (q_scaled[i] - q_unit[i] * q_inner[i])).astype(BF16),
            (k_recip[i] * (k_scaled[i] - k_unit[i] * k_inner[i])).astype(BF16),
            dv[i].astype(BF16),
        )
        for i in n
    ]
    return results, q_part, k_part


def fold(x):
    return jnp.sum(x.reshape(ROWS // 8, 8, HD), axis=0)


def row_ids():
    return lax.broadcasted_iota(jnp.int32, (ROWS, 1), 0)


def local_kernel(heads, scale, prm_ref, q_ref, k_ref, v_ref, g_ref, seg_ref, qg_ref, kg_ref, o_ref, dq_ref, dk_ref, dv_ref, sums_ref):
    me = lax.axis_index("tp")
    own = jnp.broadcast_to(seg_ref[pl.ds(me, 1), :].astype(F32), (ROWS, ROWS))
    same = own == own.T
    rows = row_ids()
    whole = jnp.logical_and(rows >= prm_ref[7], rows < ROWS - prm_ref[15])
    q_gain, k_gain = qg_ref[...], kg_ref[...]
    mean_of = averager()
    sums_ref[...] = jnp.zeros_like(sums_ref)

    def group(i, _):
        cols = [head_cols(i * BATCH + u) for u in range(BATCH)]
        items = [(q_ref[:, c], k_ref[:, c], v_ref[:, c], g_ref[:, c], same, None) for c in cols]
        results, gq, gk = units_attention(items, q_gain, k_gain, scale, mean_of)
        for c, res in zip(cols, results):
            for ref, value in zip((o_ref, dq_ref, dk_ref, dv_ref), res):
                ref[:, c] = value
        sums_ref[0:8, :] += fold(jnp.where(whole, sum(gq), 0.0))
        sums_ref[8:16, :] += fold(jnp.where(whole, sum(gk), 0.0))
        return 0

    lax.fori_loop(0, heads // BATCH, group, 0)


def cross_kernel(heads, x, prm_ref, *refs):
    own, (received, qg_ref, kg_ref, part_ref), local = refs[0:4], refs[4:8], refs[8:12]
    final, (back, gains_ref, in_pad, out_pad, sums) = refs[12:16], refs[16:]
    in_pad[ROWS : ROWS + SIZE, :] = received[...]
    for src, dst in zip(local, final):
        dst[...] = src[...]
    sums[...] = part_ref[...]
    rows = row_ids()
    cols_id = lax.broadcasted_iota(jnp.int32, (1, ROWS), 1)
    q_gain, k_gain = qg_ref[...], kg_ref[...]
    mean_of = averager()
    is_left, a_all, b_all, na, nb, h, rest = [prm_ref[8 * x + i] for i in range(7)]
    is_l = is_left == 1
    count = jnp.where(is_l, h, rest)

    def work(windows):
        items, places = [], []
        for s in range(windows):
            used = s < count
            n = jnp.where(used, jnp.where(is_l, count - 1 - s, s), 0)
            j = n + jnp.where(is_l, 0, h)
            start = jnp.where(is_l, ROWS + (n + 1) * na * BLK - ROWS, ROWS + n * nb * BLK)
            start = jnp.where(used, start, ROWS + SIZE)
            a, b = jnp.where(used, a_all, 0), jnp.where(used, b_all, 0)
            ok = jnp.logical_or(rows >= ROWS - a, rows < b)
            ok_c = jnp.logical_or(cols_id >= ROWS - a, cols_id < b)
            low = jnp.where(is_l, ROWS - a, 0)
            high = jnp.where(is_l, ROWS, b)
            theirs = jnp.logical_and(rows >= low, rows < high)
            mine = jnp.logical_and(ok, jnp.logical_not(theirs))
            cols = head_cols(j)
            window = pl.ds(pl.multiple_of(start, BLK), ROWS)
            merged = [
                jnp.where(theirs, in_pad[window, t * HD : (t + 1) * HD], ref[:, cols]) for t, ref in enumerate(own)
            ]
            items.append((*merged, jnp.logical_and(ok, ok_c), ok))
            places.append((cols, window, mine))
        results, gq, gk = units_attention(items, q_gain, k_gain, 1.0 / math.sqrt(HD), mean_of)
        for (cols, window, mine), res in zip(places, results):
            for t, (ref, value) in enumerate(zip(final, res)):
                ref[:, cols] = jnp.where(mine, value, ref[:, cols])
                out_pad[window, t * HD : (t + 1) * HD] = value
        sums[0:8, :] += fold(sum(gq))
        sums[8:16, :] += fold(sum(gk))

    @pl.when(jnp.logical_and(count > 0, count <= BATCH))
    def _():
        work(BATCH)

    @pl.when(count > BATCH)
    def _():
        work(MOST)

    back[...] = out_pad[ROWS : ROWS + SIZE, :]
    if x == 0:
        gains_ref[...] = sums[...]
        return
    both = jnp.concatenate(
        [
            jnp.sum(sums[0:8, :], axis=0, keepdims=True) / q_gain,
            jnp.sum(sums[8:16, :], axis=0, keepdims=True) / k_gain,
        ],
        axis=0,
    )
    gains_ref[...] = jnp.broadcast_to(both[None], gains_ref.shape)


def merge_kernel(heads, prm_ref, done, done2, *refs):
    local, final, pad = refs[0:4], refs[4:8], refs[8]
    step = pl.program_id(0)
    bases = (ROWS, 2 * ROWS + SIZE)

    @pl.when(step == 0)
    def _():
        for base, ref in zip(bases, (done, done2)):
            pad[base : base + SIZE, :] = ref[...]

    rows = row_ids()
    each = local[0].shape[1] // HD
    for u in range(each):
        j = step * each + u
        cols = slice(u * HD, (u + 1) * HD)
        parts = []
        for x, base in enumerate(bases):
            is_left, a, b, na, nb, h, _ = [prm_ref[8 * x + i] for i in range(7)]
            is_l = is_left == 1
            sent = jnp.where(is_l, j - h, h - 1 - j) >= 0
            n = jnp.where(sent, jnp.where(is_l, j - h, j + 1), 0)
            at = base + jnp.where(is_l, n * nb * BLK, n * na * BLK - ROWS)
            low = jnp.where(is_l, 0, ROWS - a)
            high = jnp.where(sent, jnp.where(is_l, b, ROWS), 0)
            parts.append((pl.ds(pl.multiple_of(at, BLK), ROWS), jnp.logical_and(rows >= low, rows < high)))
        for t in range(4):
            value = local[t][:, cols]
            for window, mask in parts:
                value = jnp.where(mask, pad[window, t * HD : (t + 1) * HD], value)
            final[t][:, cols] = value


def total_kernel(scale, parts_ref, after_ref, out_ref):
    out_ref[...] = jnp.sum(parts_ref[...], axis=0) * scale


VM = pl.BlockSpec(memory_space=pltpu.VMEM)
SM = pl.BlockSpec(memory_space=pltpu.SMEM)
HB = pl.BlockSpec(memory_space=pltpu.HBM)


def call(body, in_specs, out_specs, out_shape, flops, scratch=(), grid=(), vmem=40):
    return pl.pallas_call(
        body,
        grid=grid,
        in_specs=in_specs,
        out_specs=out_specs,
        out_shape=out_shape,
        scratch_shapes=list(scratch),
        compiler_params=pltpu.CompilerParams(vmem_limit_bytes=vmem * MIB),
        cost_estimate=pl.CostEstimate(flops=flops, bytes_accessed=1 << 22, transcendentals=0),
    )


def local_call(heads, args):
    rows, width = args[1].shape
    return call(
        functools.partial(local_kernel, heads, 1.0 / math.sqrt(HD)),
        [SM] + [VM] * 7,
        [VM] * 5,
        [jax.ShapeDtypeStruct((rows, width), BF16)] * 4 + [jax.ShapeDtypeStruct((16, HD), F32)],
        1 << 30,
    )(*args)


def per_device(queries, keys, values, upstream, q_gain, k_gain, segments):
    rows, width = queries.shape[1:]
    heads = width // HD
    groups, ring = lax.axis_size("grp"), lax.axis_size("tp")
    args = (queries[0], keys[0], values[0], upstream[0])
    seg = segments[0].reshape(ring, rows)
    gains = (q_gain.reshape(1, HD), k_gain.reshape(1, HD))
    full = jax.ShapeDtypeStruct((rows, width), BF16)
    sent = jax.ShapeDtypeStruct((SIZE, 4 * HD), BF16)
    part = jax.ShapeDtypeStruct((16, HD), F32)
    pad = pltpu.VMEM((SIZE + 2 * ROWS, 4 * HD), BF16)
    even, odd = [[(i, i + 1) for i in range(x, ring - 1, 2)] + [(i + 1, i) for i in range(x, ring - 1, 2)] for x in range(2)]

    out, out2, prm, *args, seg = call(
        functools.partial(pack_kernel, heads),
        [HB] * 5,
        [VM, VM, SM] + [VM] * 5,
        [sent, sent, jax.ShapeDtypeStruct((16,), jnp.int32)] + [full] * 4 + [jax.ShapeDtypeStruct(seg.shape, seg.dtype)],
        1 << 20,
        [pltpu.SemaphoreType.DMA((17,))],
        vmem=12,
    )(*[pltpu.with_memory_space_constraint(x, pltpu.HBM) for x in (*args, seg)])
    received = lax.ppermute(out, "tp", even)
    received2 = lax.ppermute(out2, "tp", odd)
    *local, sums = local_call(heads, (prm, *args, seg, *gains))

    def cross(x, received, sums, local):
        return call(
            functools.partial(cross_kernel, heads, x),
            [SM] + [VM] * 12,
            [VM] * 6,
            [full] * 4 + [sent, jax.ShapeDtypeStruct((groups, 2, HD), F32) if x else part],
            1 << 30,
            [pad, pad, pltpu.VMEM((16, HD), F32)],
        )(prm, *args, received, *gains, sums, *local)

    *merged, back, sums = cross(0, received, sums, local)
    done = lax.ppermute(back, "tp", even)
    *merged, back2, sums = cross(1, received2, sums, merged)
    done2 = lax.ppermute(back2, "tp", odd)
    sums = jnp.sum(lax.all_to_all(sums, "grp", 0, 0), axis=0)
    block = pl.BlockSpec((rows, width // 4), lambda i: (0, i))
    whole = pl.BlockSpec((SIZE, 4 * HD), lambda i: (0, 0))
    outs = call(
        functools.partial(merge_kernel, heads),
        [SM, whole, whole] + [block] * 4,
        [block] * 4,
        [full] * 4,
        1 << 20,
        [pltpu.VMEM((2 * SIZE + 3 * ROWS, 4 * HD), BF16)],
        (4,),
        16,
    )(prm, done, done2, *merged)
    sums = lax.all_to_all(jnp.broadcast_to(sums, (ring, 2, HD)), "tp", 0, 0)
    gain_grads = call(
        functools.partial(total_kernel, 1.0 / math.sqrt(groups * ring * rows * heads)),
        [VM, HB],
        VM,
        jax.ShapeDtypeStruct((2, HD), F32),
        1 << 10,
        vmem=4,
    )(sums, pltpu.with_memory_space_constraint(outs[0], pltpu.HBM))
    return tuple(x[None] for x in outs) + (gain_grads,)


def solution(mesh):
    row = P("grp", "tp", None)
    in_specs = (row, row, row, row, P(), P(), P("grp", None))
    out_specs = (row, row, row, row, P())
    return jax.shard_map(per_device, mesh=mesh, in_specs=in_specs, out_specs=out_specs, check_vma=False)
```

```python
import functools
import math

import jax
import jax.numpy as jnp
from jax import lax
from jax.experimental import pallas as pl
from jax.experimental.pallas import tpu as pltpu
from jax.sharding import PartitionSpec as P

HD = 128
ROWS = 128
BLK = 16
BATCH = 8
MOST = 12
CAP = 36
SIZE = CAP * BLK
MIB = 1024 * 1024
F32 = jnp.float32
BF16 = jnp.bfloat16


def plan(left_row, right_row, exists, heads):
    a = jnp.sum(jnp.where(left_row == right_row[:, :1], 1.0, 0.0)).astype(jnp.int32)
    b = jnp.sum(jnp.where(right_row == left_row[:, ROWS - 1 :], 1.0, 0.0)).astype(jnp.int32)
    crosses = jnp.where(jnp.logical_and(exists, a > 0), 1, 0).astype(jnp.int32)
    a, b = a * crosses, b * crosses
    na, nb = (a + BLK - 1) // BLK, (b + BLK - 1) // BLK
    h = jnp.maximum(heads // 2, heads - CAP // jnp.maximum(nb, 1))
    h = jnp.minimum(h, CAP // jnp.maximum(na, 1))
    return a, b, na, nb, h * crosses, (heads - h) * crosses


def write_plan(prm_ref, seg_ref, heads):
    me = lax.axis_index("tp")
    last = seg_ref.shape[0] - 1
    own = seg_ref[pl.ds(me, 1), :]
    prev = seg_ref[pl.ds(jnp.maximum(me - 1, 0), 1), :]
    after = seg_ref[pl.ds(jnp.minimum(me + 1, last), 1), :]
    left = plan(prev, own, me > 0, heads)
    right = plan(own, after, me < last, heads)
    both = []
    for x in range(2):
        is_left = lax.rem(me + x, 2)
        both.append([is_left] + [jnp.where(is_left == 1, p, q) for p, q in zip(left, right)])
        for i, value in enumerate(both[x]):
            prm_ref[8 * x + i] = value
    prm_ref[7] = left[1]
    prm_ref[15] = right[0]
    return both


def head_cols(j):
    return pl.ds(pl.multiple_of(j * HD, HD), HD)


def pack_kernel(heads, q_hbm, k_hbm, v_hbm, g_hbm, seg_hbm, out_ref, out_ref2, prm_ref, q_ref, k_ref, v_ref, g_ref, seg_ref, sem):
    refs = (q_ref, k_ref, v_ref, g_ref)
    step = ROWS // 4
    copies = []
    first = pltpu.make_async_copy(seg_hbm, seg_ref, sem.at[16])
    first.start()
    for t, (src, dst) in enumerate(zip((q_hbm, k_hbm, v_hbm, g_hbm), refs)):
        for r in range(4):
            part = pl.ds(r * step, step)
            copies.append(pltpu.make_async_copy(src.at[part, :], dst.at[part, :], sem.at[t * 4 + r]))
            copies[-1].start()
    first.wait()
    plans = write_plan(prm_ref, seg_ref, heads)
    for copy in copies:
        copy.wait()

    for out, (is_left, _, _, na, nb, h, rest) in zip((out_ref, out_ref2), plans):
        count = jnp.where(is_left == 1, rest, h)
        blocks = jnp.where(is_left == 1, nb, na)
        first_head = jnp.where(is_left == 1, h, 0)
        first_row = jnp.where(is_left == 1, 0, ROWS - na * BLK)

        def head(jj, _):
            cols = head_cols(first_head + jj)

            def rows(r, _):
                src = pl.ds(pl.multiple_of(first_row + r * BLK, BLK), BLK)
                dst = pl.ds(pl.multiple_of((jj * blocks + r) * BLK, BLK), BLK)
                for t, ref in enumerate(refs):
                    out[dst, t * HD : (t + 1) * HD] = ref[src, cols]
                return 0

            return lax.fori_loop(0, blocks, rows, 0)

        lax.fori_loop(0, count, head, 0)


def mm(x, y, dims):
    return lax.dot_general(x, y, (dims, ((), ())), preferred_element_type=F32)


NT = ((1,), (1,))
NN = ((1,), (0,))
TN = ((0,), (0,))


def averager():
    r = lax.broadcasted_iota(jnp.int32, (2 * HD, 2 * HD), 0) // HD
    c = lax.broadcasted_iota(jnp.int32, (2 * HD, 2 * HD), 1) // HD
    return jnp.where(r == c, 1.0 / HD, 0.0).astype(BF16)


def units_attention(items, q_gain, k_gain, scale, mean_of):
    n = range(len(items))
    q, k, v, g, mask, row_ok = zip(*items)

    def means(x, y):
        both = [mm(jnp.concatenate([x[i].astype(BF16), y[i].astype(BF16)], axis=1), mean_of, NN) for i in n]
        return [b[:, :HD] for b in both], [b[:, HD:] for b in both]

    qf, kf = [x.astype(F32) for x in q], [x.astype(F32) for x in k]
    q_mean, k_mean = means([x * x for x in qf], [x * x for x in kf])
    q_recip, k_recip = [lax.rsqrt(x + 1e-06) for x in q_mean], [lax.rsqrt(x + 1e-06) for x in k_mean]
    q_unit, k_unit = [qf[i] * q_recip[i] for i in n], [kf[i] * k_recip[i] for i in n]
    q_norm, k_norm = [(x * q_gain).astype(BF16) for x in q_unit], [(x * k_gain).astype(BF16) for x in k_unit]
    scores = [mm(q_norm[i], k_norm[i], NT) for i in n]
    weight = [
        jnp.where(mask[i], jnp.exp2(scores[i] * (scale * math.log2(math.e))), 0.0).astype(BF16) for i in n
    ]
    ones = jnp.ones((ROWS, HD), BF16)
    sums = [mm(weight[i], jnp.concatenate([v[i], ones], axis=1), NN) for i in n]
    total = [x[:, HD:] for x in sums]
    total = [t if ok is None else jnp.where(ok, t, 1.0) for t, ok in zip(total, row_ok)]
    recip = [1.0 / t for t in total]
    out = [sums[i][:, :HD] * recip[i] for i in n]
    g_part = [g[i].astype(F32) * recip[i] for i in n]
    g_both = [jnp.concatenate([g_part[i].astype(BF16), (g_part[i] * out[i]).astype(BF16)], axis=1) for i in n]
    dprobs = [mm(g_both[i], jnp.concatenate([v[i], -ones], axis=1), NT) for i in n]
    dscores = [(weight[i].astype(F32) * dprobs[i]).astype(BF16) for i in n]
    dv = [mm(weight[i], g_both[i][:, :HD], TN) for i in n]
    dq = [mm(dscores[i], k_norm[i], NN) for i in n]
    dk = [mm(dscores[i], q_norm[i], TN) for i in n]
    q_scaled, k_scaled = [x * (q_gain * scale) for x in dq], [x * (k_gain * scale) for x in dk]
    q_part, k_part = [q_scaled[i] * q_unit[i] for i in n], [k_scaled[i] * k_unit[i] for i in n]
    q_inner, k_inner = means(q_part, k_part)
    results = [
        (
            out[i].astype(BF16),
            (q_recip[i] * (q_scaled[i] - q_unit[i] * q_inner[i])).astype(BF16),
            (k_recip[i] * (k_scaled[i] - k_unit[i] * k_inner[i])).astype(BF16),
            dv[i].astype(BF16),
        )
        for i in n
    ]
    return results, q_part, k_part


def fold(x):
    return jnp.sum(x.reshape(ROWS // 8, 8, HD), axis=0)


def row_ids():
    return lax.broadcasted_iota(jnp.int32, (ROWS, 1), 0)


def local_kernel(heads, scale, prm_ref, q_ref, k_ref, v_ref, g_ref, seg_ref, qg_ref, kg_ref, o_ref, dq_ref, dk_ref, dv_ref, sums_ref):
    me = lax.axis_index("tp")
    own = jnp.broadcast_to(seg_ref[pl.ds(me, 1), :].astype(F32), (ROWS, ROWS))
    same = own == own.T
    rows = row_ids()
    whole = jnp.logical_and(rows >= prm_ref[7], rows < ROWS - prm_ref[15])
    q_gain, k_gain = qg_ref[...], kg_ref[...]
    mean_of = averager()
    sums_ref[...] = jnp.zeros_like(sums_ref)

    def group(i, _):
        cols = [head_cols(i * BATCH + u) for u in range(BATCH)]
        items = [(q_ref[:, c], k_ref[:, c], v_ref[:, c], g_ref[:, c], same, None) for c in cols]
        results, gq, gk = units_attention(items, q_gain, k_gain, scale, mean_of)
        for c, res in zip(cols, results):
            for ref, value in zip((o_ref, dq_ref, dk_ref, dv_ref), res):
                ref[:, c] = value
        sums_ref[0:8, :] += fold(jnp.where(whole, sum(gq), 0.0))
        sums_ref[8:16, :] += fold(jnp.where(whole, sum(gk), 0.0))
        return 0

    lax.fori_loop(0, heads // BATCH, group, 0)


def cross_kernel(heads, x, prm_ref, *refs):
    own, (received, qg_ref, kg_ref, part_ref), local = refs[0:4], refs[4:8], refs[8:12]
    final, (back, gains_ref, in_pad, out_pad, sums) = refs[12:16], refs[16:]
    in_pad[ROWS : ROWS + SIZE, :] = received[...]
    for src, dst in zip(local, final):
        dst[...] = src[...]
    sums[...] = part_ref[...]
    rows = row_ids()
    cols_id = lax.broadcasted_iota(jnp.int32, (1, ROWS), 1)
    q_gain, k_gain = qg_ref[...], kg_ref[...]
    mean_of = averager()
    is_left, a_all, b_all, na, nb, h, rest = [prm_ref[8 * x + i] for i in range(7)]
    is_l = is_left == 1
    count = jnp.where(is_l, h, rest)

    def work(windows):
        items, places = [], []
        for s in range(windows):
            used = s < count
            n = jnp.where(used, jnp.where(is_l, count - 1 - s, s), 0)
            j = n + jnp.where(is_l, 0, h)
            start = jnp.where(is_l, ROWS + (n + 1) * na * BLK - ROWS, ROWS + n * nb * BLK)
            start = jnp.where(used, start, ROWS + SIZE)
            a, b = jnp.where(used, a_all, 0), jnp.where(used, b_all, 0)
            ok = jnp.logical_or(rows >= ROWS - a, rows < b)
            ok_c = jnp.logical_or(cols_id >= ROWS - a, cols_id < b)
            low = jnp.where(is_l, ROWS - a, 0)
            high = jnp.where(is_l, ROWS, b)
            theirs = jnp.logical_and(rows >= low, rows < high)
            mine = jnp.logical_and(ok, jnp.logical_not(theirs))
            cols = head_cols(j)
            window = pl.ds(pl.multiple_of(start, BLK), ROWS)
            merged = [
                jnp.where(theirs, in_pad[window, t * HD : (t + 1) * HD], ref[:, cols]) for t, ref in enumerate(own)
            ]
            items.append((*merged, jnp.logical_and(ok, ok_c), ok))
            places.append((cols, window, mine))
        results, gq, gk = units_attention(items, q_gain, k_gain, 1.0 / math.sqrt(HD), mean_of)
        for (cols, window, mine), res in zip(places, results):
            for t, (ref, value) in enumerate(zip(final, res)):
                ref[:, cols] = jnp.where(mine, value, ref[:, cols])
                out_pad[window, t * HD : (t + 1) * HD] = value
        sums[0:8, :] += fold(sum(gq))
        sums[8:16, :] += fold(sum(gk))

    @pl.when(jnp.logical_and(count > 0, count <= BATCH))
    def _():
        work(BATCH)

    @pl.when(count > BATCH)
    def _():
        work(MOST)

    back[...] = out_pad[ROWS : ROWS + SIZE, :]
    if x == 0:
        gains_ref[...] = sums[...]
        return
    both = jnp.concatenate(
        [
            jnp.sum(sums[0:8, :], axis=0, keepdims=True) / q_gain,
            jnp.sum(sums[8:16, :], axis=0, keepdims=True) / k_gain,
        ],
        axis=0,
    )
    gains_ref[...] = jnp.broadcast_to(both[None], gains_ref.shape)


def merge_kernel(heads, prm_ref, done, done2, *refs):
    local, final, pad = refs[0:4], refs[4:8], refs[8]
    step = pl.program_id(0)
    bases = (ROWS, 2 * ROWS + SIZE)

    @pl.when(step == 0)
    def _():
        for base, ref in zip(bases, (done, done2)):
            pad[base : base + SIZE, :] = ref[...]

    rows = row_ids()
    each = local[0].shape[1] // HD
    for u in range(each):
        j = step * each + u
        cols = slice(u * HD, (u + 1) * HD)
        parts = []
        for x, base in enumerate(bases):
            is_left, a, b, na, nb, h, _ = [prm_ref[8 * x + i] for i in range(7)]
            is_l = is_left == 1
            sent = jnp.where(is_l, j - h, h - 1 - j) >= 0
            n = jnp.where(sent, jnp.where(is_l, j - h, j + 1), 0)
            at = base + jnp.where(is_l, n * nb * BLK, n * na * BLK - ROWS)
            low = jnp.where(is_l, 0, ROWS - a)
            high = jnp.where(sent, jnp.where(is_l, b, ROWS), 0)
            parts.append((pl.ds(pl.multiple_of(at, BLK), ROWS), jnp.logical_and(rows >= low, rows < high)))
        for t in range(4):
            value = local[t][:, cols]
            for window, mask in parts:
                value = jnp.where(mask, pad[window, t * HD : (t + 1) * HD], value)
            final[t][:, cols] = value


def total_kernel(scale, parts_ref, after_ref, out_ref):
    out_ref[...] = jnp.sum(parts_ref[...], axis=0) * scale


VM = pl.BlockSpec(memory_space=pltpu.VMEM)
SM = pl.BlockSpec(memory_space=pltpu.SMEM)
HB = pl.BlockSpec(memory_space=pltpu.HBM)


def call(body, in_specs, out_specs, out_shape, flops, scratch=(), grid=(), vmem=40):
    return pl.pallas_call(
        body,
        grid=grid,
        in_specs=in_specs,
        out_specs=out_specs,
        out_shape=out_shape,
        scratch_shapes=list(scratch),
        compiler_params=pltpu.CompilerParams(vmem_limit_bytes=vmem * MIB),
        cost_estimate=pl.CostEstimate(flops=flops, bytes_accessed=1 << 22, transcendentals=0),
    )


def local_call(heads, args):
    rows, width = args[1].shape
    return call(
        functools.partial(local_kernel, heads, 1.0 / math.sqrt(HD)),
        [SM] + [VM] * 7,
        [VM] * 5,
        [jax.ShapeDtypeStruct((rows, width), BF16)] * 4 + [jax.ShapeDtypeStruct((16, HD), F32)],
        1 << 30,
    )(*args)


def per_device(queries, keys, values, upstream, q_gain, k_gain, segments):
    rows, width = queries.shape[1:]
    heads = width // HD
    groups, ring = lax.axis_size("grp"), lax.axis_size("tp")
    args = (queries[0], keys[0], values[0], upstream[0])
    seg = segments[0].reshape(ring, rows)
    gains = (q_gain.reshape(1, HD), k_gain.reshape(1, HD))
    full = jax.ShapeDtypeStruct((rows, width), BF16)
    sent = jax.ShapeDtypeStruct((SIZE, 4 * HD), BF16)
    part = jax.ShapeDtypeStruct((16, HD), F32)
    pad = pltpu.VMEM((SIZE + 2 * ROWS, 4 * HD), BF16)
    even, odd = [[(i, i + 1) for i in range(x, ring - 1, 2)] + [(i + 1, i) for i in range(x, ring - 1, 2)] for x in range(2)]

    out, out2, prm, *args, seg = call(
        functools.partial(pack_kernel, heads),
        [HB] * 5,
        [VM, VM, SM] + [VM] * 5,
        [sent, sent, jax.ShapeDtypeStruct((16,), jnp.int32)] + [full] * 4 + [jax.ShapeDtypeStruct(seg.shape, seg.dtype)],
        1 << 20,
        [pltpu.SemaphoreType.DMA((17,))],
        vmem=12,
    )(*[pltpu.with_memory_space_constraint(x, pltpu.HBM) for x in (*args, seg)])
    received = lax.ppermute(out, "tp", even)
    received2 = lax.ppermute(out2, "tp", odd)
    *local, sums = local_call(heads, (prm, *args, seg, *gains))

    def cross(x, received, sums, local):
        return call(
            functools.partial(cross_kernel, heads, x),
            [SM] + [VM] * 12,
            [VM] * 6,
            [full] * 4 + [sent, jax.ShapeDtypeStruct((groups, 2, HD), F32) if x else part],
            1 << 30,
            [pad, pad, pltpu.VMEM((16, HD), F32)],
        )(prm, *args, received, *gains, sums, *local)

    *merged, back, sums = cross(0, received, sums, local)
    done = lax.ppermute(back, "tp", even)
    *merged, back2, sums = cross(1, received2, sums, merged)
    done2 = lax.ppermute(back2, "tp", odd)
    sums = jnp.sum(lax.all_to_all(sums, "grp", 0, 0), axis=0)
    block = pl.BlockSpec((rows, width // 4), lambda i: (0, i))
    whole = pl.BlockSpec((SIZE, 4 * HD), lambda i: (0, 0))
    outs = call(
        functools.partial(merge_kernel, heads),
        [SM, whole, whole] + [block] * 4,
        [block] * 4,
        [full] * 4,
        1 << 20,
        [pltpu.VMEM((2 * SIZE + 3 * ROWS, 4 * HD), BF16)],
        (4,),
        16,
    )(prm, *[pltpu.with_memory_space_constraint(x, pltpu.HBM) for x in (done, done2)], *merged)
    sums = lax.all_to_all(jnp.broadcast_to(sums, (ring, 2, HD)), "tp", 0, 0)
    gain_grads = call(
        functools.partial(total_kernel, 1.0 / math.sqrt(groups * ring * rows * heads)),
        [VM, HB],
        VM,
        jax.ShapeDtypeStruct((2, HD), F32),
        1 << 10,
        vmem=4,
    )(sums, pltpu.with_memory_space_constraint(outs[0], pltpu.HBM))
    return tuple(x[None] for x in outs) + (gain_grads,)


def solution(mesh):
    row = P("grp", "tp", None)
    in_specs = (row, row, row, row, P(), P(), P("grp", None))
    out_specs = (row, row, row, row, P())
    return jax.shard_map(per_device, mesh=mesh, in_specs=in_specs, out_specs=out_specs, check_vma=False)
```

```python
import functools
import math

import jax
import jax.numpy as jnp
from jax import lax
from jax.experimental import pallas as pl
from jax.experimental.pallas import tpu as pltpu
from jax.sharding import PartitionSpec as P

HD = 128
ROWS = 128
BLK = 16
BATCH = 8
MOST = 12
CAP = 36
SIZE = CAP * BLK
NONE = -1e30
MIB = 1024 * 1024
F32 = jnp.float32
BF16 = jnp.bfloat16


def plan(left_row, right_row, exists, heads):
    a = jnp.sum(jnp.where(left_row == right_row[:, :1], 1.0, 0.0)).astype(jnp.int32)
    b = jnp.sum(jnp.where(right_row == left_row[:, ROWS - 1 :], 1.0, 0.0)).astype(jnp.int32)
    crosses = jnp.where(jnp.logical_and(exists, a > 0), 1, 0).astype(jnp.int32)
    a, b = a * crosses, b * crosses
    na, nb = (a + BLK - 1) // BLK, (b + BLK - 1) // BLK
    h = jnp.maximum(heads // 2, heads - CAP // jnp.maximum(nb, 1))
    h = jnp.minimum(h, CAP // jnp.maximum(na, 1))
    return a, b, na, nb, h * crosses, (heads - h) * crosses


def write_plan(prm_ref, seg_ref, heads):
    me = lax.axis_index("tp")
    last = seg_ref.shape[0] - 1
    own = seg_ref[pl.ds(me, 1), :]
    prev = seg_ref[pl.ds(jnp.maximum(me - 1, 0), 1), :]
    after = seg_ref[pl.ds(jnp.minimum(me + 1, last), 1), :]
    left = plan(prev, own, me > 0, heads)
    right = plan(own, after, me < last, heads)
    both = []
    for x in range(2):
        is_left = lax.rem(me + x, 2)
        both.append([is_left] + [jnp.where(is_left == 1, p, q) for p, q in zip(left, right)])
        for i, value in enumerate(both[x]):
            prm_ref[8 * x + i] = value
    prm_ref[7] = left[1]
    prm_ref[15] = right[0]
    return both


def head_cols(j):
    return pl.ds(pl.multiple_of(j * HD, HD), HD)


def pack(out_ref, values, refs):
    is_left, _, _, na, nb, h, rest = values
    count = jnp.where(is_left == 1, rest, h)
    blocks = jnp.where(is_left == 1, nb, na)
    first_head = jnp.where(is_left == 1, h, 0)
    first_row = jnp.where(is_left == 1, 0, ROWS - na * BLK)

    def head(jj, _):
        cols = head_cols(first_head + jj)

        def rows(r, _):
            src = pl.ds(pl.multiple_of(first_row + r * BLK, BLK), BLK)
            dst = pl.ds(pl.multiple_of((jj * blocks + r) * BLK, BLK), BLK)
            for t, ref in enumerate(refs):
                out_ref[dst, t * HD : (t + 1) * HD] = ref[src, cols]
            return 0

        return lax.fori_loop(0, blocks, rows, 0)

    lax.fori_loop(0, count, head, 0)


def pack_kernel(heads, q_hbm, k_hbm, v_hbm, g_hbm, seg_hbm, out_ref, prm_ref, q_ref, k_ref, v_ref, g_ref, seg_ref, sem):
    refs = (q_ref, k_ref, v_ref, g_ref)
    step = ROWS // 4
    copies = []
    first = pltpu.make_async_copy(seg_hbm, seg_ref, sem.at[16])
    first.start()
    for t, (src, dst) in enumerate(zip((q_hbm, k_hbm, v_hbm, g_hbm), refs)):
        for r in range(4):
            part = pl.ds(r * step, step)
            copies.append(pltpu.make_async_copy(src.at[part, :], dst.at[part, :], sem.at[t * 4 + r]))
            copies[-1].start()
    first.wait()
    plans = write_plan(prm_ref, seg_ref, heads)
    for copy in copies:
        copy.wait()

    pack(out_ref, plans[0], refs)


def pack_odd_kernel(prm_ref, q_ref, k_ref, v_ref, g_ref, out_ref):
    pack(out_ref, [prm_ref[8 + i] for i in range(7)], (q_ref, k_ref, v_ref, g_ref))


def mm(x, y, dims):
    return lax.dot_general(x, y, (dims, ((), ())), preferred_element_type=F32)


NT = ((1,), (1,))
NN = ((1,), (0,))
TN = ((0,), (0,))


def averager():
    r = lax.broadcasted_iota(jnp.int32, (2 * HD, 2 * HD), 0) // HD
    c = lax.broadcasted_iota(jnp.int32, (2 * HD, 2 * HD), 1) // HD
    return jnp.where(r == c, 1.0 / HD, 0.0).astype(BF16)


def units_attention(items, q_gain, k_gain, scale, mean_of):
    n = range(len(items))
    q, k, v, g, bias, row_ok = zip(*items)

    def means(x, y):
        both = [mm(jnp.concatenate([x[i].astype(BF16), y[i].astype(BF16)], axis=1), mean_of, NN) for i in n]
        return [b[:, :HD] for b in both], [b[:, HD:] for b in both]

    qf, kf = [x.astype(F32) for x in q], [x.astype(F32) for x in k]
    q_mean, k_mean = means([x * x for x in qf], [x * x for x in kf])
    q_recip, k_recip = [lax.rsqrt(x + 1e-06) for x in q_mean], [lax.rsqrt(x + 1e-06) for x in k_mean]
    q_unit, k_unit = [qf[i] * q_recip[i] for i in n], [kf[i] * k_recip[i] for i in n]
    q_norm, k_norm = [(x * q_gain).astype(BF16) for x in q_unit], [(x * k_gain).astype(BF16) for x in k_unit]
    scores = [mm(q_norm[i], k_norm[i], NT) for i in n]
    weight = [jnp.exp2(scores[i] * (scale * math.log2(math.e)) + bias[i]).astype(BF16) for i in n]
    ones = jnp.ones((ROWS, HD), BF16)
    sums = [mm(weight[i], jnp.concatenate([v[i], ones], axis=1), NN) for i in n]
    total = [x[:, HD:] for x in sums]
    total = [t if ok is None else jnp.where(ok, t, 1.0) for t, ok in zip(total, row_ok)]
    recip = [1.0 / t for t in total]
    out = [sums[i][:, :HD] * recip[i] for i in n]
    g_part = [g[i].astype(F32) * recip[i] for i in n]
    g_both = [jnp.concatenate([g_part[i].astype(BF16), (g_part[i] * out[i]).astype(BF16)], axis=1) for i in n]
    dprobs = [mm(g_both[i], jnp.concatenate([v[i], -ones], axis=1), NT) for i in n]
    dscores = [(weight[i].astype(F32) * dprobs[i]).astype(BF16) for i in n]
    dv = [mm(weight[i], g_both[i][:, :HD], TN) for i in n]
    dq = [mm(dscores[i], k_norm[i], NN) for i in n]
    dk = [mm(dscores[i], q_norm[i], TN) for i in n]
    q_scaled, k_scaled = [x * (q_gain * scale) for x in dq], [x * (k_gain * scale) for x in dk]
    q_part, k_part = [q_scaled[i] * q_unit[i] for i in n], [k_scaled[i] * k_unit[i] for i in n]
    q_inner, k_inner = means(q_part, k_part)
    results = [
        (
            out[i].astype(BF16),
            (q_recip[i] * (q_scaled[i] - q_unit[i] * q_inner[i])).astype(BF16),
            (k_recip[i] * (k_scaled[i] - k_unit[i] * k_inner[i])).astype(BF16),
            dv[i].astype(BF16),
        )
        for i in n
    ]
    return results, q_part, k_part


def fold(x):
    return jnp.sum(x.reshape(ROWS // 8, 8, HD), axis=0)


def row_ids():
    return lax.broadcasted_iota(jnp.int32, (ROWS, 1), 0)


def local_kernel(heads, scale, prm_ref, q_ref, k_ref, v_ref, g_ref, seg_ref, qg_ref, kg_ref, o_ref, dq_ref, dk_ref, dv_ref, sums_ref):
    me = lax.axis_index("tp")
    own = jnp.broadcast_to(seg_ref[pl.ds(me, 1), :].astype(F32), (ROWS, ROWS))
    same = jnp.where(own == own.T, 0.0, NONE)
    rows = row_ids()
    whole = jnp.logical_and(rows >= prm_ref[7], rows < ROWS - prm_ref[15])
    q_gain, k_gain = qg_ref[...], kg_ref[...]
    mean_of = averager()
    sums_ref[...] = jnp.zeros_like(sums_ref)

    def group(i, _):
        cols = [head_cols(i * BATCH + u) for u in range(BATCH)]
        items = [(q_ref[:, c], k_ref[:, c], v_ref[:, c], g_ref[:, c], same, None) for c in cols]
        results, gq, gk = units_attention(items, q_gain, k_gain, scale, mean_of)
        for c, res in zip(cols, results):
            for ref, value in zip((o_ref, dq_ref, dk_ref, dv_ref), res):
                ref[:, c] = value
        sums_ref[0:8, :] += fold(jnp.where(whole, sum(gq), 0.0))
        sums_ref[8:16, :] += fold(jnp.where(whole, sum(gk), 0.0))
        return 0

    lax.fori_loop(0, heads // BATCH, group, 0)


def cross_kernel(heads, x, prm_ref, *refs):
    own, (received, qg_ref, kg_ref, part_ref), local = refs[0:4], refs[4:8], refs[8:12]
    final, (back, gains_ref, in_pad, out_pad, sums) = refs[12:16], refs[16:]
    in_pad[ROWS : ROWS + SIZE, :] = received[...]
    for src, dst in zip(local, final):
        dst[...] = src[...]
    sums[...] = part_ref[...]
    rows = row_ids()
    cols_id = lax.broadcasted_iota(jnp.int32, (1, ROWS), 1)
    q_gain, k_gain = qg_ref[...], kg_ref[...]
    mean_of = averager()
    is_left, a_all, b_all, na, nb, h, rest = [prm_ref[8 * x + i] for i in range(7)]
    is_l = is_left == 1
    count = jnp.where(is_l, h, rest)

    def work(windows):
        items, places = [], []
        for s in range(windows):
            used = s < count
            n = jnp.where(used, jnp.where(is_l, count - 1 - s, s), 0)
            j = n + jnp.where(is_l, 0, h)
            start = jnp.where(is_l, ROWS + (n + 1) * na * BLK - ROWS, ROWS + n * nb * BLK)
            start = jnp.where(used, start, ROWS + SIZE)
            a, b = jnp.where(used, a_all, 0), jnp.where(used, b_all, 0)
            ok = jnp.logical_or(rows >= ROWS - a, rows < b)
            ok_c = jnp.logical_or(cols_id >= ROWS - a, cols_id < b)
            low = jnp.where(is_l, ROWS - a, 0)
            high = jnp.where(is_l, ROWS, b)
            theirs = jnp.logical_and(rows >= low, rows < high)
            mine = jnp.logical_and(ok, jnp.logical_not(theirs))
            cols = head_cols(j)
            window = pl.ds(pl.multiple_of(start, BLK), ROWS)
            merged = [
                jnp.where(theirs, in_pad[window, t * HD : (t + 1) * HD], ref[:, cols]) for t, ref in enumerate(own)
            ]
            merged[3] = jnp.where(ok, merged[3], jnp.zeros_like(merged[3]))
            items.append((*merged, jnp.where(ok_c, 0.0, NONE), ok))
            places.append((cols, window, mine))
        results, gq, gk = units_attention(items, q_gain, k_gain, 1.0 / math.sqrt(HD), mean_of)
        for (cols, window, mine), res in zip(places, results):
            for t, (ref, value) in enumerate(zip(final, res)):
                ref[:, cols] = jnp.where(mine, value, ref[:, cols])
                out_pad[window, t * HD : (t + 1) * HD] = value
        sums[0:8, :] += fold(sum(gq))
        sums[8:16, :] += fold(sum(gk))

    @pl.when(jnp.logical_and(count > 0, count <= BATCH))
    def _():
        work(BATCH)

    @pl.when(count > BATCH)
    def _():
        work(MOST)

    back[...] = out_pad[ROWS : ROWS + SIZE, :]
    if x == 0:
        gains_ref[...] = sums[...]
        return
    both = jnp.concatenate(
        [
            jnp.sum(sums[0:8, :], axis=0, keepdims=True) / q_gain,
            jnp.sum(sums[8:16, :], axis=0, keepdims=True) / k_gain,
        ],
        axis=0,
    )
    gains_ref[...] = jnp.broadcast_to(both[None], gains_ref.shape)


def merge_kernel(heads, prm_ref, done, done2, *refs):
    local, final, pad = refs[0:4], refs[4:8], refs[8]
    step = pl.program_id(0)
    bases = (ROWS, 2 * ROWS + SIZE)

    @pl.when(step == 0)
    def _():
        for base, ref in zip(bases, (done, done2)):
            pad[base : base + SIZE, :] = ref[...]

    rows = row_ids()
    each = local[0].shape[1] // HD
    for u in range(each):
        j = step * each + u
        cols = slice(u * HD, (u + 1) * HD)
        parts = []
        for x, base in enumerate(bases):
            is_left, a, b, na, nb, h, _ = [prm_ref[8 * x + i] for i in range(7)]
            is_l = is_left == 1
            sent = jnp.where(is_l, j - h, h - 1 - j) >= 0
            n = jnp.where(sent, jnp.where(is_l, j - h, j + 1), 0)
            at = base + jnp.where(is_l, n * nb * BLK, n * na * BLK - ROWS)
            low = jnp.where(is_l, 0, ROWS - a)
            high = jnp.where(sent, jnp.where(is_l, b, ROWS), 0)
            parts.append((pl.ds(pl.multiple_of(at, BLK), ROWS), jnp.logical_and(rows >= low, rows < high)))
        for t in range(4):
            value = local[t][:, cols]
            for window, mask in parts:
                value = jnp.where(mask, pad[window, t * HD : (t + 1) * HD], value)
            final[t][:, cols] = value


def total_kernel(scale, parts_ref, after_ref, out_ref):
    out_ref[...] = jnp.sum(parts_ref[...], axis=0) * scale


VM = pl.BlockSpec(memory_space=pltpu.VMEM)
SM = pl.BlockSpec(memory_space=pltpu.SMEM)
HB = pl.BlockSpec(memory_space=pltpu.HBM)


def call(body, in_specs, out_specs, out_shape, flops, scratch=(), grid=(), vmem=40):
    return pl.pallas_call(
        body,
        grid=grid,
        in_specs=in_specs,
        out_specs=out_specs,
        out_shape=out_shape,
        scratch_shapes=list(scratch),
        compiler_params=pltpu.CompilerParams(vmem_limit_bytes=vmem * MIB),
        cost_estimate=pl.CostEstimate(flops=flops, bytes_accessed=1 << 22, transcendentals=0),
    )


def local_call(heads, args):
    rows, width = args[1].shape
    return call(
        functools.partial(local_kernel, heads, 1.0 / math.sqrt(HD)),
        [SM] + [VM] * 7,
        [VM] * 5,
        [jax.ShapeDtypeStruct((rows, width), BF16)] * 4 + [jax.ShapeDtypeStruct((16, HD), F32)],
        1 << 30,
    )(*args)


def per_device(queries, keys, values, upstream, q_gain, k_gain, segments):
    rows, width = queries.shape[1:]
    heads = width // HD
    groups, ring = lax.axis_size("grp"), lax.axis_size("tp")
    args = (queries[0], keys[0], values[0], upstream[0])
    seg = segments[0].reshape(ring, rows)
    gains = (q_gain.reshape(1, HD), k_gain.reshape(1, HD))
    full = jax.ShapeDtypeStruct((rows, width), BF16)
    sent = jax.ShapeDtypeStruct((SIZE, 4 * HD), BF16)
    part = jax.ShapeDtypeStruct((16, HD), F32)
    pad = pltpu.VMEM((SIZE + 2 * ROWS, 4 * HD), BF16)
    even, odd = [[(i, i + 1) for i in range(x, ring - 1, 2)] + [(i + 1, i) for i in range(x, ring - 1, 2)] for x in range(2)]

    out, prm, *args, seg = call(
        functools.partial(pack_kernel, heads),
        [HB] * 5,
        [VM, SM] + [VM] * 5,
        [sent, jax.ShapeDtypeStruct((16,), jnp.int32)] + [full] * 4 + [jax.ShapeDtypeStruct(seg.shape, seg.dtype)],
        1 << 20,
        [pltpu.SemaphoreType.DMA((17,))],
        vmem=12,
    )(*[pltpu.with_memory_space_constraint(x, pltpu.HBM) for x in (*args, seg)])
    received = lax.ppermute(out, "tp", even)
    out2 = call(pack_odd_kernel, [SM] + [VM] * 4, VM, sent, 1 << 20, vmem=12)(prm, *args)
    received2 = lax.ppermute(out2, "tp", odd)
    *local, sums = local_call(heads, (prm, *args, seg, *gains))

    def cross(x, received, sums, local):
        return call(
            functools.partial(cross_kernel, heads, x),
            [SM] + [VM] * 12,
            [VM] * 6,
            [full] * 4 + [sent, jax.ShapeDtypeStruct((groups, 2, HD), F32) if x else part],
            1 << 30,
            [pad, pad, pltpu.VMEM((16, HD), F32)],
        )(prm, *args, received, *gains, sums, *local)

    *merged, back, sums = cross(0, received, sums, local)
    done = lax.ppermute(back, "tp", even)
    *merged, back2, sums = cross(1, received2, sums, merged)
    done2 = lax.ppermute(back2, "tp", odd)
    sums = jnp.sum(lax.all_to_all(sums, "grp", 0, 0), axis=0)
    block = pl.BlockSpec((rows, width // 4), lambda i: (0, i))
    whole = pl.BlockSpec((SIZE, 4 * HD), lambda i: (0, 0))
    outs = call(
        functools.partial(merge_kernel, heads),
        [SM, whole, whole] + [block] * 4,
        [block] * 4,
        [full] * 4,
        1 << 20,
        [pltpu.VMEM((2 * SIZE + 3 * ROWS, 4 * HD), BF16)],
        (4,),
        16,
    )(prm, *[pltpu.with_memory_space_constraint(x, pltpu.HBM) for x in (done, done2)], *merged)
    sums = lax.all_to_all(jnp.broadcast_to(sums, (ring, 2, HD)), "tp", 0, 0)
    gain_grads = call(
        functools.partial(total_kernel, 1.0 / math.sqrt(groups * ring * rows * heads)),
        [VM, HB],
        VM,
        jax.ShapeDtypeStruct((2, HD), F32),
        1 << 10,
        vmem=4,
    )(sums, pltpu.with_memory_space_constraint(outs[0], pltpu.HBM))
    return tuple(x[None] for x in outs) + (gain_grads,)


def solution(mesh):
    row = P("grp", "tp", None)
    in_specs = (row, row, row, row, P(), P(), P("grp", None))
    out_specs = (row, row, row, row, P())
    return jax.shard_map(per_device, mesh=mesh, in_specs=in_specs, out_specs=out_specs, check_vma=False)
```
